32 devices in a mesh: mem: 2 (over core), tile: 16 (over z, y, x).
Axes of the slice: x: 2, y: 2, z: 4, core: 2. Of those that a mesh axis runs over, the one named last changes fastest.
Arguments:
- anomalies: bfloat16 [64, 256, 512], P('tile', 'mem'), may hold values from -6 to 6
- innovations: bfloat16 [128, 256, 512], P('tile', 'mem'), may hold values from -3 to 3
- obs_tile: int32 [128], P('tile'), may hold values from 0 to 63, as said below
- pair_tiles: int32 [128, 2], P('tile'), may hold values from 0 to 63, as said below
- loc_bin: int32 [128], P('tile'), may hold values from 0 to 4
Outputs:
- analysis: bfloat16 [64, 256, 512], P('tile', 'mem')
The draws below stay inside these ranges and needn't reach their ends.
Inputs may be any that keep to these rules, and one draw needn't show every extreme that they name: Block o lies in a tile of its own index of tile: obs_tile[o] // 4 == o // 8. `pair_tiles`: slot k's first tile i has i // 4 == k // 8; its second tile j differs from i and j // 4 - i // 4 lies in 0 to 2, equal to 2 for some slot. Pairs may repeat. `loc_bin`: bin 4 marks an empty slot.
All inputs are finite; a program needn't handle non-finite values.
Results may differ from the reference program's by a relative error of at most 0.0051.
Values may be sent and summed in bfloat16 or wider, within the bound.
No kernel may reach another device: no remote copies, remote signals or barrier semaphores. Data moves between devices by JAX's collectives and lax.ppermute only.
A program may use at most 128 MiB of HBM per device.

```python
import jax
import jax.numpy as jnp
from jax import lax

MEMBERS = 256
POINTS = 512
TILE_DEV = 4
HOPS = 2
NBIN = 4
RADIUS = 4
PAIR_DEV = 8
OBS_DEV = 8
TILES = 64
PAIRS = 128
OBS = 128


def draw_obs_tile(key, part):
    rows = jnp.arange(OBS, dtype=jnp.int32)
    device = rows // OBS_DEV
    local = jax.random.randint(key, (OBS,), 0, TILE_DEV, dtype=jnp.int32)
    local = jnp.where(rows % OBS_DEV == 0, TILE_DEV - 1, local)
    return device * TILE_DEV + local


def draw_pair_tiles(key, part):
    devices_all = TILES // TILE_DEV
    rows = jnp.arange(PAIRS, dtype=jnp.int32)
    device = rows // PAIR_DEV
    slot = rows % PAIR_DEV
    key_first, key_step, key_far, key_near = jax.random.split(key, 4)
    first_local = jax.random.randint(key_first, (PAIRS,), 0, TILE_DEV, dtype=jnp.int32)
    first_local = jnp.where(jnp.logical_and(device == devices_all - 1, slot == 1), TILE_DEV - 1, first_local)
    step = jax.random.randint(key_step, (PAIRS,), 0, HOPS + 1, dtype=jnp.int32)
    step = jnp.where(slot == 0, HOPS, step)
    step = jnp.where(device + step >= devices_all, 0, step)
    far_local = jax.random.randint(key_far, (PAIRS,), 0, TILE_DEV, dtype=jnp.int32)
    near_local = (first_local + 1 + jax.random.randint(key_near, (PAIRS,), 0, TILE_DEV - 1, dtype=jnp.int32)) % TILE_DEV
    second_local = jnp.where(step == 0, near_local, far_local)
    first = device * TILE_DEV + first_local
    second = (device + step) * TILE_DEV + second_local
    return jnp.stack([first, second], axis=1)


def place_ends(drawn, key, least, largest):
    dims = drawn.shape
    spot = [jax.random.randint(jax.random.fold_in(key, axis), (), 0, dims[axis]) for axis in range(len(dims))]
    drawn = drawn.at[tuple(spot)].set(least)
    longest = dims.index(max(dims))
    spot[longest] = (spot[longest] + 1) % dims[longest]
    return drawn.at[tuple(spot)].set(largest)


def block_scale(rng, dims, cuts, smallest, largest):
    factor_of, own = 1.0, jax.random.fold_in(rng, 6)
    for position, blocks in cuts:
        heights = jnp.exp(jax.random.uniform(jax.random.fold_in(own, position), (blocks,), jnp.float32, smallest / len(cuts), largest / len(cuts)))
        factor_of = factor_of * jnp.repeat(heights, dims[position] // blocks).reshape([-1 if axis == position else 1 for axis in range(len(dims))])
    return factor_of


def bell_draw(stream_key, extent, spread, limit, cuts=(), held_as=jnp.bfloat16):
    drawn = jax.random.normal(stream_key, extent, jnp.float32) * spread
    if len(cuts) > 0:
        drawn = block_scale(stream_key, extent, cuts, -0.22, 0.18) * drawn
    return jnp.clip(drawn, min=-limit, max=limit).astype(held_as)


def setup_inputs(seed: int = 0) -> dict:
    key_of = jax.random.split(jax.random.key(seed), 6)
    anomalies = bell_draw(key_of[0], (TILES, MEMBERS, POINTS), 1.0, 6.0, ((0, 16), (1, 2)))
    innovations = bell_draw(key_of[1], (OBS, MEMBERS, POINTS), 0.5, 3.0, ((0, 16), (1, 2)))
    obs_tile = draw_obs_tile(jax.random.fold_in(key_of[5], 71), 0)
    pair_tiles = draw_pair_tiles(jax.random.fold_in(key_of[5], 71), 0)
    loc_bin = place_ends(jax.random.randint(key_of[4], (PAIRS,), 0, NBIN + 1), jax.random.fold_in(key_of[4], 1), 0, NBIN).astype(jnp.int32)
    return dict(anomalies=anomalies, innovations=innovations, obs_tile=obs_tile, pair_tiles=pair_tiles, loc_bin=loc_bin)


def weights_for(bins, points):
    positions = jnp.arange(points, dtype=jnp.int32)
    column = (positions % 32).astype(jnp.float32)
    levels = (positions // 32).astype(jnp.float32)
    along = 0.5 * RADIUS * bins.astype(jnp.float32)[:, None, None] + column[None, None, :] - column[None, :, None]
    across = levels[None, None, :] - levels[None, :, None]
    weight = jnp.exp(-(along * along + across * across) / (2.0 * RADIUS * RADIUS))
    return jnp.where(bins[:, None, None] < NBIN, weight, 0.0)


def reference(anomalies, innovations, obs_tile, pair_tiles, loc_bin):
    tiles_all = anomalies.shape[0]
    points = anomalies.shape[2]
    onehot = (obs_tile[:, None] == jnp.arange(tiles_all, dtype=jnp.int32)[None, :]).astype(jnp.float32)
    forcing = jnp.einsum("ot,omp->tmp", onehot, innovations.astype(jnp.float32)).astype(jnp.bfloat16)
    zero_bin = weights_for(jnp.zeros((1,), jnp.int32), points)[0]

    def self_term(tile_index):
        block = anomalies[tile_index]
        cross = jnp.dot(block.T, block, preferred_element_type=jnp.float32)
        own = (zero_bin * cross / (MEMBERS - 1)).astype(jnp.bfloat16)
        return jnp.dot(forcing[tile_index], own.T, preferred_element_type=jnp.float32)

    increment = lax.map(self_term, jnp.arange(tiles_all, dtype=jnp.int32))

    def pair_step(total, slot):
        first = slot[0]
        second = slot[1]
        bin_value = slot[2]
        cross = jnp.dot(anomalies[first].T, anomalies[second], preferred_element_type=jnp.float32)
        covar = (weights_for(bin_value[None], points)[0] * cross / (MEMBERS - 1)).astype(jnp.bfloat16)
        to_first = jnp.dot(forcing[second], covar.T, preferred_element_type=jnp.float32)
        to_second = jnp.dot(forcing[first], covar, preferred_element_type=jnp.float32)
        total = total.at[first].add(to_first)
        total = total.at[second].add(to_second)
        return total, None

    slots = jnp.concatenate([pair_tiles.astype(jnp.int32), loc_bin.astype(jnp.int32)[:, None]], axis=1)
    increment, _ = lax.scan(pair_step, increment, slots)
    return (anomalies.astype(jnp.float32) + increment).astype(jnp.bfloat16)
```

```python
import jax
import jax.numpy as jnp
from jax import lax
from jax.experimental import pallas as pl
from jax.experimental.pallas import tpu as pltpu
from jax.sharding import PartitionSpec as P

MEMBERS = 256
NBIN = 4
RADIUS = 4
WIDTH = 32
ROWS = 128
GROUPS = 3
F32 = jnp.float32
BF16 = jnp.bfloat16
VMEM_BYTES = 40 * 1024 * 1024


def routes(size):
    to_u, to_v = [], []
    for t in range(size):
        r = t % 4
        if r != 3:
            to_u.append((t, t + (1, 2, -2)[r]))
        if r != 1:
            to_v.append((t, t + {0: -4, 2: 1, 3: 2}[r]))
    inside = lambda pairs: [(a, b) for a, b in pairs if 0 <= a < size and 0 <= b < size]
    return inside(to_u), inside(to_v)


def back(pairs):
    return [(b, a) for a, b in pairs]


def entries_for(codes, place, tiles):
    r = place % 4
    out = []
    for group, code in enumerate(codes):
        left = code - 1
        bins = left % NBIN
        left = left // NBIN
        first = left % tiles
        left = left // tiles
        second = left % tiles
        dist = left // tiles
        if group == 0:
            other = jnp.where(dist == 0, 0, jnp.where((dist == 2) & (r == 0), 1, -1))
        elif group == 1:
            at_0 = jnp.where(dist == 2, 2, -1)
            at_1 = jnp.where(dist == 1, 0, -1)
            at_3 = jnp.where(dist == 1, 2, jnp.where(dist == 2, 0, -1))
            other = jnp.where(r == 0, at_0, jnp.where(r == 1, at_1, jnp.where(r == 3, at_3, -1)))
        else:
            at_1 = jnp.where(dist == 1, 1, jnp.where(dist == 2, 0, -1))
            at_3 = jnp.where(dist == 1, 0, -1)
            other = jnp.where(r == 1, at_1, jnp.where(r == 3, at_3, -1))
        entry = 1 + bins + NBIN * (group * tiles + first + GROUPS * tiles * (other * tiles + second))
        out.append(jnp.where((code > 0) & (other >= 0), entry, 0))
    return jnp.concatenate(out)


def decode(entry, tiles):
    left = entry - 1
    bins = lax.rem(left, NBIN)
    left = lax.div(left, NBIN)
    return bins, lax.rem(left, GROUPS * tiles), lax.div(left, GROUPS * tiles)


def fill_weights(along, across, points):
    q = lax.broadcasted_iota(jnp.int32, (WIDTH, points), 1) % WIDTH
    p = lax.broadcasted_iota(jnp.int32, (WIDTH, points), 0)
    gap = (q - p).astype(F32)
    for b in range(NBIN):
        shift = gap + 0.5 * RADIUS * b
        along[b] = jnp.exp(-(shift * shift) / (2.0 * RADIUS * RADIUS))
    levels = points // WIDTH
    row = lax.broadcasted_iota(jnp.int32, (levels, points), 1) // WIDTH
    level = lax.broadcasted_iota(jnp.int32, (levels, points), 0)
    gap = (row - level).astype(F32)
    across[...] = jnp.exp(-(gap * gap) / (2.0 * RADIUS * RADIUS)) / (MEMBERS - 1)


def covariance(a, first, second, bins, along, across, put):
    points = a.shape[2]
    right = a[second]
    weight = along[bins]
    for p0 in range(0, points, ROWS):
        cross = lax.dot_general(
            a[first, :, pl.ds(p0, ROWS)], right, (((0,), (0,)), ((), ())), preferred_element_type=F32
        )
        for k in range(ROWS // WIDTH):
            level = (p0 // WIDTH) + k
            part = cross[k * WIDTH : (k + 1) * WIDTH]
            put(p0 + k * WIDTH, (part * (weight * across[pl.ds(level, 1), :])).astype(BF16))


def to_first(g, c):
    return lax.dot_general(g, c, (((1,), (1,)), ((), ())), preferred_element_type=F32)


def to_second(g, c):
    return lax.dot_general(g, c, (((1,), (0,)), ((), ())), preferred_element_type=F32)


def load_groups(halves, a, sems):
    tiles, members = halves[0].shape[0], halves[0].shape[1]
    copies = []
    for k, half in enumerate(halves):
        copy = pltpu.make_async_copy(
            half, a.at[pl.ds((k // 2) * tiles, tiles), pl.ds((k % 2) * members, members), :], sems.at[k]
        )
        copy.start()
        copies.append(copy)
    return copies


def put_in(ref):
    def put(row, value):
        ref[pl.ds(row, WIDTH), :] = value

    return put


def forcing_kernel(obs, innov, out, total):
    total[...] = jnp.zeros_like(total)

    def step(o, carry):
        t = obs[o]
        total[t] = total[t] + innov[o].astype(F32)
        return carry

    lax.fori_loop(0, innov.shape[0], step, 0)
    out[...] = total[...].astype(BF16)


def local_kernel(entries, mine, theirs, g, out, a, c, along, across, sems):
    tiles, points = mine.shape[0], mine.shape[2]
    copies = load_groups([mine, theirs], a, sems)
    fill_weights(along, across, points)
    for copy in copies:
        copy.wait()

    def own(t, carry):
        covariance(a, t, t, 0, along, across, put_in(c))
        out[t] = to_first(g[t], c[...])
        return carry

    lax.fori_loop(0, tiles, own, 0)

    def pair(k, carry):
        entry = entries[k]
        bins, first, second = decode(entry, tiles)

        @pl.when((entry > 0) & (second < tiles))
        def _():
            covariance(a, first, second, bins, along, across, put_in(c))
            out[first] = out[first] + to_first(g[second], c[...])
            out[second] = out[second] + to_second(g[first], c[...])

        return carry

    lax.fori_loop(0, entries.shape[0] // GROUPS, pair, 0)


def early_kernel(entries, lm, lt, um, ut, vm, vt, g, far, inc, a, c, along, across, sems):
    tiles, points = lm.shape[0], lm.shape[2]
    copies = load_groups([lm, lt, um, ut, vm, vt], a, sems)
    fill_weights(along, across, points)
    inc[...] = jnp.zeros_like(inc)
    for copy in copies:
        copy.wait()
    slots = entries.shape[0] // GROUPS

    def pair(k, carry):
        entry = entries[k]
        bins, first, second = decode(entry, tiles)
        local_first, local_second = first < tiles, second < tiles

        @pl.when((entry > 0) & jnp.logical_not(local_first) & jnp.logical_not(local_second))
        def _():
            covariance(a, first, second, bins, along, across, put_in(far.at[lax.rem(k, slots)]))

        @pl.when((entry > 0) & (local_first != local_second))
        def _():
            covariance(a, first, second, bins, along, across, put_in(c))

            @pl.when(local_first)
            def _():
                inc[second - tiles] = inc[second - tiles] + to_second(g[first], c[...])

            @pl.when(local_second)
            def _():
                inc[first - tiles] = inc[first - tiles] + to_first(g[second], c[...])

        return carry

    lax.fori_loop(0, entries.shape[0], pair, 0)


def far_kernel(entries, far, inc, gu, gv, to_u, to_v, total, g):
    tiles = gu.shape[0]
    slots = entries.shape[0] // GROUPS
    total[...] = inc[...]
    g[pl.ds(0, tiles)] = gu[...]
    g[pl.ds(tiles, tiles)] = gv[...]

    def pair(k, carry):
        entry = entries[slots + k]
        _, first, second = decode(entry, tiles)

        @pl.when((entry > 0) & (first >= tiles) & (second >= tiles))
        def _():
            c = far[lax.rem(k, slots)]
            i, j = first - tiles, second - tiles
            total[i] = total[i] + to_first(g[j], c)
            total[j] = total[j] + to_second(g[i], c)

        return carry

    lax.fori_loop(0, 2 * slots, pair, 0)
    to_u[...] = total[pl.ds(0, tiles)].astype(BF16)
    to_v[...] = total[pl.ds(tiles, tiles)].astype(BF16)


def late_kernel(entries, lm, lt, um, ut, vm, vt, gu, gv, base, out, a, g, c, along, across, sems):
    tiles, points = lm.shape[0], lm.shape[2]
    copies = load_groups([lm, lt, um, ut, vm, vt], a, sems)
    fill_weights(along, across, points)
    g[pl.ds(0, tiles)] = gu[...]
    g[pl.ds(tiles, tiles)] = gv[...]
    for copy in copies:
        copy.wait()
    out[...] = base[...] + a[pl.ds(0, tiles), pl.ds(0, lm.shape[1]), :].astype(F32)

    def pair(k, carry):
        entry = entries[k]
        bins, first, second = decode(entry, tiles)
        local_first, local_second = first < tiles, second < tiles

        @pl.when((entry > 0) & (local_first != local_second))
        def _():
            covariance(a, first, second, bins, along, across, put_in(c))

            @pl.when(local_first)
            def _():
                out[first] = out[first] + to_first(g[second - tiles], c[...])

            @pl.when(local_second)
            def _():
                out[second] = out[second] + to_second(g[first - tiles], c[...])

        return carry

    lax.fori_loop(0, entries.shape[0], pair, 0)


def final_kernel(total, from_u, from_v, out):
    out[...] = (total[...] + from_u[...].astype(F32) + from_v[...].astype(F32)).astype(BF16)


def call(kernel, outs, places, scratch, us, *args):
    spec = {"s": pl.BlockSpec(memory_space=pltpu.SMEM), "v": pl.BlockSpec(memory_space=pltpu.VMEM), "h": pl.BlockSpec(memory_space=pl.ANY)}
    return pl.pallas_call(
        kernel,
        out_shape=outs,
        in_specs=[spec[p] for p in places],
        out_specs=jax.tree.map(lambda _: spec["v"], outs),
        scratch_shapes=scratch,
        compiler_params=pltpu.CompilerParams(vmem_limit_bytes=VMEM_BYTES),
        cost_estimate=pl.CostEstimate(flops=int(us * 1e9), bytes_accessed=int(us * 3e6), transcendentals=0),
    )(*args)


def per_device(anomalies, innovations, obs_tile, pair_tiles, loc_bin):
    tiles, members, points = anomalies.shape
    slots = loc_bin.shape[0]
    size = lax.axis_size("tile")
    place = lax.axis_index("tile")
    base = place * tiles
    to_u, to_v = routes(size)
    send = lambda x, pairs: lax.ppermute(x, "tile", pairs)
    swap = lambda x: lax.ppermute(x, "mem", [(0, 1), (1, 0)])

    a_u = send(anomalies, to_u)
    a_v = send(anomalies, to_v)
    a_t = swap(anomalies)
    first = pair_tiles[:, 0] - base
    second = pair_tiles[:, 1] - base
    code = 1 + loc_bin + NBIN * (first + tiles * second)
    code = jnp.where(loc_bin < NBIN, code, 0)
    entries = entries_for((code, send(code, to_u), send(code, to_v)), place, tiles)

    sds = jax.ShapeDtypeStruct
    vm = pltpu.VMEM
    weights = [vm((NBIN, WIDTH, points), F32), vm((points // WIDTH, points), F32)]
    forcing = call(
        forcing_kernel, sds(anomalies.shape, BF16), "sv", [vm(anomalies.shape, F32)], 1, obs_tile - base, innovations
    )
    g_u = send(forcing, to_u)
    g_v = send(forcing, to_v)
    a_ut = swap(a_u)
    a_vt = swap(a_v)

    local = call(
        local_kernel,
        sds(anomalies.shape, F32),
        "shhv",
        [vm((tiles, 2 * members, points), BF16), vm((points, points), BF16), *weights, pltpu.SemaphoreType.DMA((2,))],
        5,
        entries,
        anomalies,
        a_t,
        forcing,
    )
    groups = vm((GROUPS * tiles, 2 * members, points), BF16)
    square = vm((points, points), BF16)
    far, inc = call(
        early_kernel,
        (sds((slots, points, points), BF16), sds((2 * tiles, members, points), F32)),
        "shhhhhhv",
        [groups, square, *weights, pltpu.SemaphoreType.DMA((6,))],
        6,
        entries,
        anomalies,
        a_t,
        a_u,
        a_ut,
        a_v,
        a_vt,
        forcing,
    )
    inc_u, inc_v = call(
        far_kernel,
        (sds(anomalies.shape, BF16), sds(anomalies.shape, BF16)),
        "svvvv",
        [vm((2 * tiles, members, points), F32), vm((2 * tiles, members, points), BF16)],
        2,
        entries,
        far,
        inc,
        g_u,
        g_v,
    )
    from_u = send(inc_u, back(to_u))
    from_v = send(inc_v, back(to_v))
    total = call(
        late_kernel,
        sds(anomalies.shape, F32),
        "shhhhhhvvv",
        [groups, vm((2 * tiles, members, points), BF16), square, *weights, pltpu.SemaphoreType.DMA((6,))],
        6,
        entries,
        anomalies,
        a_t,
        a_u,
        a_ut,
        a_v,
        a_vt,
        g_u,
        g_v,
        local,
    )
    return call(final_kernel, sds(anomalies.shape, BF16), "vvv", [], 1, total, from_u, from_v)


def solution(mesh):
    return jax.shard_map(
        per_device,
        mesh=mesh,
        in_specs=(
            P("tile", "mem", None),
            P("tile", "mem", None),
            P("tile"),
            P("tile", None),
            P("tile"),
        ),
        out_specs=P("tile", "mem", None),
        check_vma=False,
    )
```

```python
import jax
import jax.numpy as jnp
from jax import lax
from jax.experimental import pallas as pl
from jax.experimental.pallas import tpu as pltpu
from jax.sharding import PartitionSpec as P

MEMBERS = 256
NBIN = 4
RADIUS = 4
WIDTH = 32
ROWS = 128
GROUPS = 3
F32 = jnp.float32
BF16 = jnp.bfloat16
VMEM_BYTES = 24 * 1024 * 1024
FULL_BYTES = 60 * 1024 * 1024

FROM_U = {0: 1, 1: 2, 2: 2}
FROM_V = {0: 2, 1: 4, 2: 1}


def routes(size, steps):
    return [(t + step, t) for t in range(size) for r, step in steps.items() if t % 4 == r and t + step < size]


def back(pairs):
    return [(b, a) for a, b in pairs]


def entries_for(lists, place, tiles):
    r = place % 4
    out = []
    for group, (code, second) in enumerate(lists):
        left = code - 1
        bins = left % NBIN
        first = left // NBIN
        dist = second // tiles
        second = second % tiles
        if group == 0:
            at_0 = dist
            at_1 = jnp.where(dist == 2, 1, -1)
            at_2 = 3 - dist
            other = jnp.where(r == 0, at_0, jnp.where(r == 1, at_1, jnp.where(r == 2, at_2, -1)))
            other = jnp.where(dist == 0, 0, other)
        elif group == 1:
            other = jnp.where(((r == 0) & (dist == 1)) | ((r == 1) & (dist == 2)), 2, -1)
        else:
            other = jnp.where((r == 2) & (dist == 1), 1, -1)
        entry = 1 + bins + NBIN * (group * tiles + first + GROUPS * tiles * (other * tiles + second))
        out.append(jnp.where((code > 0) & (other >= 0), entry, 0))
    return jnp.concatenate(out)


def decode(entry, tiles):
    left = entry - 1
    bins = lax.rem(left, NBIN)
    left = lax.div(left, NBIN)
    return bins, lax.rem(left, GROUPS * tiles), lax.div(left, GROUPS * tiles)


def fill_weights(along, across, points):
    q = lax.broadcasted_iota(jnp.int32, (WIDTH, points), 1) % WIDTH
    p = lax.broadcasted_iota(jnp.int32, (WIDTH, points), 0)
    gap = (q - p).astype(F32)
    for b in range(NBIN):
        shift = gap + 0.5 * RADIUS * b
        along[b] = jnp.exp(-(shift * shift) / (2.0 * RADIUS * RADIUS))
    levels = points // WIDTH
    row = lax.broadcasted_iota(jnp.int32, (levels, points), 1) // WIDTH
    level = lax.broadcasted_iota(jnp.int32, (levels, points), 0)
    gap = (row - level).astype(F32)
    across[...] = jnp.exp(-(gap * gap) / (2.0 * RADIUS * RADIUS)) / (MEMBERS - 1)


def both(a, tile, cols):
    tiles = a.shape[1]
    half, t = 2 * lax.div(tile, tiles), lax.rem(tile, tiles)
    return jnp.concatenate([a[half, t, :, cols], a[half + 1, t, :, cols]], axis=0)


def covariance(a, first, second, bins, along, across, put):
    points = a.shape[3]
    right = both(a, second, slice(None))
    weight = along[bins]
    for p0 in range(0, points, ROWS):
        cross = lax.dot_general(
            both(a, first, slice(p0, p0 + ROWS)), right, (((0,), (0,)), ((), ())), preferred_element_type=F32
        )
        for k in range(ROWS // WIDTH):
            level = (p0 // WIDTH) + k
            part = cross[k * WIDTH : (k + 1) * WIDTH]
            put(p0 + k * WIDTH, (part * (weight * across[pl.ds(level, 1), :])).astype(BF16))


def to_first(g, c):
    return lax.dot_general(g, c, (((1,), (1,)), ((), ())), preferred_element_type=F32)


def to_second(g, c):
    return lax.dot_general(g, c, (((1,), (0,)), ((), ())), preferred_element_type=F32)


def load_groups(messages, a, sems):
    copies = []
    for k, message in enumerate(messages):
        copy = pltpu.make_async_copy(message, a.at[k], sems.at[k])
        copy.start()
        copies.append(copy)
    return copies


def put_in(ref):
    def put(row, value):
        ref[pl.ds(row, WIDTH), :] = value

    return put


def forcing_kernel(obs, innov, out, total):
    tiles = out.shape[0]
    total[...] = jnp.zeros_like(total)

    def step(o, carry):
        t = lax.rem(obs[o], tiles)
        total[t] = total[t] + innov[o].astype(F32)
        return carry

    lax.fori_loop(0, innov.shape[0], step, 0)
    out[...] = total[...].astype(BF16)


def early_kernel(entries, lm, lt, um, ut, vm, vt, g, far, inc, a, c, along, across, sems):
    tiles, points = g.shape[0], g.shape[2]
    copies = load_groups([lm, lt, um, ut, vm, vt], a, sems)
    fill_weights(along, across, points)
    inc[...] = jnp.zeros_like(inc)
    for copy in copies:
        copy.wait()
    slots = entries.shape[0] // GROUPS

    def pair(k, carry):
        entry = entries[k]
        bins, first, second = decode(entry, tiles)
        local_first, local_second = first < tiles, second < tiles

        @pl.when((entry > 0) & jnp.logical_not(local_first))
        def _():
            covariance(a, first, second, bins, along, across, put_in(far.at[lax.rem(k, slots)]))

        @pl.when((entry > 0) & local_first & jnp.logical_not(local_second))
        def _():
            covariance(a, first, second, bins, along, across, put_in(c))
            inc[second - tiles] = inc[second - tiles] + to_second(g[first], c[...])

        return carry

    lax.fori_loop(0, entries.shape[0], pair, 0)


def far_kernel(entries, far, inc, gu, gv, to_u, to_v, total):
    del inc
    tiles = gu.shape[0]
    slots = entries.shape[0] // GROUPS

    def pair(k, carry):
        entry = entries[slots + k]
        _, first, second = decode(entry, tiles)
        far_pair = (entry > 0) & (first >= tiles) & (second >= tiles)

        def add(g_first, g_second):
            c = far.at[lax.rem(k, slots)]
            i, j = first - tiles, second - tiles
            total[i] = total[i] + to_first(g_second[lax.rem(j, tiles)], c[...])
            total[j] = total[j] + to_second(g_first[lax.rem(i, tiles)], c[...])

        @pl.when(far_pair & (first < second))
        def _():
            add(gu, gv)

        @pl.when(far_pair & (first > second))
        def _():
            add(gv, gu)

        return carry

    lax.fori_loop(0, 2 * slots, pair, 0)
    to_u[...] = total[pl.ds(0, tiles)].astype(BF16)
    to_v[...] = total[pl.ds(tiles, tiles)].astype(BF16)


def late_kernel(entries, lm, lt, um, ut, vm, vt, g_l, gu, gv, out, a, g, c, along, across, sems):
    tiles, members, points = g_l.shape
    copies = load_groups([lm, lt, um, ut, vm, vt], a, sems)
    fill_weights(along, across, points)
    g[pl.ds(0, tiles)] = g_l[...]
    g[pl.ds(tiles, tiles)] = gu[...]
    g[pl.ds(2 * tiles, tiles)] = gv[...]
    for copy in copies:
        copy.wait()

    def own(t, carry):
        covariance(a, t, t, 0, along, across, put_in(c))
        out[t] = a[0, t].astype(F32) + to_first(g[t], c[...])
        return carry

    lax.fori_loop(0, tiles, own, 0)

    def pair(k, carry):
        entry = entries[k]
        bins, first, second = decode(entry, tiles)

        @pl.when((entry > 0) & (first < tiles))
        def _():
            covariance(a, first, second, bins, along, across, put_in(c))
            out[first] = out[first] + to_first(g[second], c[...])

            @pl.when(second < tiles)
            def _():
                out[second] = out[second] + to_second(g[first], c[...])

        return carry

    lax.fori_loop(0, entries.shape[0] // GROUPS, pair, 0)


def final_kernel(total, from_u, from_v, out):
    out[...] = (total[...] + from_u[...].astype(F32) + from_v[...].astype(F32)).astype(BF16)


def call(kernel, outs, places, scratch, us, *args, aliases={}, grant=VMEM_BYTES):
    spec = {"s": pl.BlockSpec(memory_space=pltpu.SMEM), "v": pl.BlockSpec(memory_space=pltpu.VMEM), "h": pl.BlockSpec(memory_space=pl.ANY), "d": pl.BlockSpec(memory_space=pltpu.HBM)}
    return pl.pallas_call(
        kernel,
        out_shape=outs,
        in_specs=[spec[p] for p in places],
        out_specs=jax.tree.map(lambda _: spec["v"], outs),
        scratch_shapes=scratch,
        input_output_aliases=aliases,
        compiler_params=pltpu.CompilerParams(vmem_limit_bytes=grant),
        cost_estimate=pl.CostEstimate(flops=int(us * 1e7), bytes_accessed=int(us * 3e4), transcendentals=0),
    )(*args)


def per_device(anomalies, innovations, obs_tile, pair_tiles, loc_bin):
    tiles, members, points = anomalies.shape
    slots = loc_bin.shape[0]
    size = lax.axis_size("tile")
    place = lax.axis_index("tile")
    to_u, to_v = routes(size, FROM_U), routes(size, FROM_V)
    send = lambda x, pairs: lax.ppermute(x, "tile", pairs)
    swap = lambda x: lax.ppermute(x, "mem", [(0, 1), (1, 0)])

    sds = jax.ShapeDtypeStruct
    vm = pltpu.VMEM
    a_v = send(anomalies, to_v)
    a_u = send(anomalies, to_u)
    a_t = swap(anomalies)
    innovations, pair_tiles, a_t = lax.optimization_barrier((innovations, pair_tiles, a_t))
    first = pair_tiles[:, 0] % tiles
    second = pair_tiles[:, 1] - pair_tiles[:, 0] + first
    slot_list = jnp.stack([jnp.where(loc_bin < NBIN, 1 + loc_bin + NBIN * first, 0), second])
    lists = (slot_list, send(slot_list, to_u), send(slot_list, to_v))
    weights = [vm((NBIN, WIDTH, points), F32), vm((points // WIDTH, points), F32)]
    forcing = call(
        forcing_kernel, sds(anomalies.shape, BF16), "sv", [vm(anomalies.shape, F32)], 1, obs_tile, innovations
    )
    g_v = send(forcing, to_v)
    g_u = send(forcing, to_u)
    entries = entries_for(lists, place, tiles)
    a_ut = swap(a_u)
    a_vt = swap(a_v)

    groups = vm((2 * GROUPS, *anomalies.shape), BF16)
    square = vm((points, points), BF16)
    far, inc = call(
        early_kernel,
        (sds((slots, points, points), BF16), sds((2 * tiles, members, points), F32)),
        "shhhhhhv",
        [groups, square, *weights, pltpu.SemaphoreType.DMA((2 * GROUPS,))],
        6,
        entries,
        anomalies,
        a_t,
        a_u,
        a_ut,
        a_v,
        a_vt,
        forcing,
    )
    inc_u, inc_v, _ = call(
        far_kernel,
        (sds(anomalies.shape, BF16), sds(anomalies.shape, BF16), sds(inc.shape, F32)),
        "svvvv",
        [],
        2,
        entries,
        far,
        inc,
        g_u,
        g_v,
        aliases={2: 2},
    )
    from_v = send(inc_v, back(to_v))
    from_u = send(inc_u, back(to_u))
    total = call(
        late_kernel,
        sds(anomalies.shape, F32),
        "shhhhhhvvv",
        [groups, vm((GROUPS * tiles, members, points), BF16), square, *weights, pltpu.SemaphoreType.DMA((2 * GROUPS,))],
        10,
        entries,
        anomalies,
        a_t,
        a_u,
        a_ut,
        a_v,
        a_vt,
        forcing,
        g_u,
        g_v,
    )
    return call(final_kernel, sds(anomalies.shape, BF16), "vvv", [], 1, total, from_u, from_v)


def solution(mesh):
    return jax.shard_map(
        per_device,
        mesh=mesh,
        in_specs=(
            P("tile", "mem", None),
            P("tile", "mem", None),
            P("tile"),
            P("tile", None),
            P("tile"),
        ),
        out_specs=P("tile", "mem", None),
        check_vma=False,
    )
```

```python
import functools

import jax
import jax.numpy as jnp
from jax import lax
from jax.experimental import pallas as pl
from jax.experimental.pallas import tpu as pltpu
from jax.sharding import PartitionSpec as P

MEMBERS = 256
NBIN = 4
RADIUS = 4
WIDTH = 32
ROWS = 128
SLOT_ROWS = 16
GROUPS = 3
F32 = jnp.float32
BF16 = jnp.bfloat16
VMEM_BYTES = 24 * 1024 * 1024
FULL_BYTES = 60 * 1024 * 1024

FROM_U = {0: 1, 1: 2, 2: 2}
FROM_V = {0: 2, 1: 4, 2: 1}


def routes(size, steps):
    return [(t + step, t) for t in range(size) for r, step in steps.items() if t % 4 == r and t + step < size]


def back(pairs):
    return [(b, a) for a, b in pairs]


def slot_codes(message, slots):
    rows = message.shape[0] - SLOT_ROWS
    parts = message[rows : rows + slots, :3].astype(jnp.int32)
    return parts[:, 0] + (parts[:, 1] << 8) + (parts[:, 2] << 16)


def entries_for(own, other, place, tiles):
    r = place % 4
    out = []
    for foreign, code in enumerate((own, other)):
        first, second = (code >> 8) & 255, code >> 16
        dist = second // tiles
        if foreign:
            first_group = jnp.where(r == 2, 2, 1)
            second_group = jnp.where(dist == jnp.where(r == 1, 2, 1), 3 - first_group, -1)
            second_group = jnp.where(r == 3, -1, second_group)
        else:
            first_group = 0
            second_group = jnp.where(r == 0, dist, jnp.where(r == 2, 3 - dist, jnp.where((r == 1) & (dist == 2), 1, -1)))
            second_group = jnp.where(dist == 0, 0, second_group)
        entry = (code & 255) + ((first + tiles * first_group) << 8) + ((second % tiles + tiles * second_group) << 16)
        out.append(jnp.where((code > 0) & (second_group >= 0), entry, 0))
    return jnp.concatenate(out)


def decode(entry):
    return lax.shift_right_logical(entry, 1) & 127, lax.shift_right_logical(entry, 8) & 255, lax.shift_right_logical(entry, 16)


def fill_weights(along, across, points):
    q = lax.broadcasted_iota(jnp.int32, (WIDTH, points), 1) % WIDTH
    p = lax.broadcasted_iota(jnp.int32, (WIDTH, points), 0)
    gap = (q - p).astype(F32)
    for b in range(NBIN):
        shift = gap + 0.5 * RADIUS * b
        along[b] = jnp.exp(-(shift * shift) / (2.0 * RADIUS * RADIUS))
    levels = points // WIDTH
    row = lax.broadcasted_iota(jnp.int32, (levels, points), 1) // WIDTH
    level = lax.broadcasted_iota(jnp.int32, (levels, points), 0)
    gap = (row - level).astype(F32)
    across[...] = jnp.exp(-(gap * gap) / (2.0 * RADIUS * RADIUS)) / (MEMBERS - 1)


def both(a, tile, cols):
    tiles = (a.shape[1] - SLOT_ROWS) // ROWS
    half = 2 * lax.div(tile, tiles)
    rows = pl.ds(pl.multiple_of(lax.rem(tile, tiles) * ROWS, ROWS), ROWS)
    return jnp.concatenate([a[half, rows, cols], a[half + 1, rows, cols]], axis=0)


def covariance(a, first, second, bins, along, across, put):
    points = a.shape[2]
    right = both(a, second, slice(None))
    weight = along[bins]
    for p0 in range(0, points, ROWS):
        cross = lax.dot_general(
            both(a, first, slice(p0, p0 + ROWS)), right, (((0,), (0,)), ((), ())), preferred_element_type=F32
        )
        for k in range(ROWS // WIDTH):
            level = (p0 // WIDTH) + k
            part = cross[k * WIDTH : (k + 1) * WIDTH]
            put(p0 + k * WIDTH, (part * (weight * across[pl.ds(level, 1), :])).astype(BF16))


def to_first(g, c):
    return lax.dot_general(g, c, (((1,), (1,)), ((), ())), preferred_element_type=F32)


def to_second(g, c):
    return lax.dot_general(g, c, (((1,), (0,)), ((), ())), preferred_element_type=F32)


def load_groups(messages, a, sems):
    copies = []
    for k, message in enumerate(messages):
        copy = pltpu.make_async_copy(message, a.at[k], sems.at[k])
        copy.start()
        copies.append(copy)
    return copies


def put_in(ref):
    def put(row, value):
        ref[pl.ds(row, WIDTH), :] = value

    return put


def pack_kernel(pairs, bins, anomalies, out, pairs_s, bins_s, sems):
    tiles, members = anomalies.shape[0], anomalies.shape[1]
    slots = bins.shape[0]
    copies = [pltpu.make_async_copy(pairs, pairs_s, sems.at[tiles]), pltpu.make_async_copy(bins, bins_s, sems.at[tiles + 1])]
    for t in range(tiles):
        copies.append(pltpu.make_async_copy(anomalies.at[t], out.at[pl.ds(t * members, members), :], sems.at[t]))
    for copy in copies:
        copy.start()
    copies[0].wait()
    copies[1].wait()
    row = lax.broadcasted_iota(jnp.int32, (SLOT_ROWS, 128), 0)
    lane = lax.broadcasted_iota(jnp.int32, (SLOT_ROWS, 128), 1)
    value = jnp.zeros(lane.shape, jnp.int32)
    for k in range(slots):
        first = lax.rem(pairs_s[0, k], tiles)
        second = pairs_s[1, k] - pairs_s[0, k] + first
        parts = jnp.where(lane == 0, 1 + 2 * bins_s[k], jnp.where(lane == 1, first, jnp.where(lane == 2, second, 0)))
        value = jnp.where((row == k) & (bins_s[k] < NBIN), parts, value)
    out[pl.ds(tiles * members, SLOT_ROWS), :] = jnp.zeros((SLOT_ROWS, out.shape[1]), BF16)
    out[pl.ds(tiles * members, SLOT_ROWS), pl.ds(0, 128)] = value.astype(F32).astype(BF16)
    for copy in copies[2:]:
        copy.wait()


def forcing_kernel(obs, innov, out, total):
    tiles = out.shape[0]
    total[...] = jnp.zeros_like(total)

    def step(o, carry):
        t = lax.rem(obs[o], tiles)
        total[t] = total[t] + innov[o].astype(F32)
        return carry

    lax.fori_loop(0, innov.shape[0], step, 0)
    out[...] = total[...].astype(BF16)


def early_kernel(entries, lm, lt, um, ut, vm, vt, g, far, inc_u, inc_v, a, c, along, across, sems):
    tiles, points = g.shape[0], g.shape[2]
    copies = load_groups([lm, lt, um, ut, vm, vt], a, sems)
    fill_weights(along, across, points)
    inc_u[...] = jnp.zeros_like(inc_u)
    inc_v[...] = jnp.zeros_like(inc_v)
    for copy in copies:
        copy.wait()
    slots = entries.shape[0] // 2

    def pair(k, carry):
        entry = entries[k]
        bins, first, second = decode(entry)
        local_first, local_second = first < tiles, second < tiles

        @pl.when((entry > 0) & jnp.logical_not(local_first))
        def _():
            covariance(a, first, second, bins, along, across, put_in(far.at[lax.rem(k, slots)]))

        @pl.when((entry > 0) & local_first & jnp.logical_not(local_second))
        def _():
            covariance(a, first, second, bins, along, across, put_in(c))
            part = to_second(g[first], c[...])

            @pl.when(second < 2 * tiles)
            def _():
                inc_u[second - tiles] = inc_u[second - tiles] + part

            @pl.when(second >= 2 * tiles)
            def _():
                inc_v[second - 2 * tiles] = inc_v[second - 2 * tiles] + part


        return carry

    lax.fori_loop(0, entries.shape[0], pair, 0)


def far_kernel(group, entries, far, inc, g, out, total):
    tiles = g.shape[0]
    slots = entries.shape[0] // 2
    total[...] = inc[...]

    def pair(k, carry):
        entry = entries[slots + k]
        _, first, second = decode(entry)
        here, there = group * tiles, (3 - group) * tiles
        first_here = (first >= here) & (first < here + tiles)

        @pl.when((entry > 0) & first_here)
        def _():
            total[first - here] = total[first - here] + to_first(g[second - there], far[k])

        @pl.when((entry > 0) & jnp.logical_not(first_here))
        def _():
            total[second - here] = total[second - here] + to_second(g[first - there], far[k])

        return carry

    lax.fori_loop(0, slots, pair, 0)
    out[...] = total[...].astype(BF16)


def late_kernel(entries, lm, lt, um, ut, vm, vt, g_l, gu, gv, out, a, g, c, along, across, sems):
    tiles, members, points = g_l.shape
    copies = load_groups([lm, lt, um, ut, vm, vt], a, sems)
    fill_weights(along, across, points)
    g[pl.ds(0, tiles)] = g_l[...]
    g[pl.ds(tiles, tiles)] = gu[...]
    g[pl.ds(2 * tiles, tiles)] = gv[...]
    for copy in copies:
        copy.wait()

    def own(t, carry):
        covariance(a, t, t, 0, along, across, put_in(c))
        out[t] = a[0, pl.ds(pl.multiple_of(t * members, members), members), :].astype(F32) + to_first(g[t], c[...])
        return carry

    lax.fori_loop(0, tiles, own, 0)

    def pair(k, carry):
        entry = entries[k]
        bins, first, second = decode(entry)

        @pl.when((entry > 0) & (first < tiles))
        def _():
            covariance(a, first, second, bins, along, across, put_in(c))
            out[first] = out[first] + to_first(g[second], c[...])

            @pl.when(second < tiles)
            def _():
                out[second] = out[second] + to_second(g[first], c[...])

        return carry

    lax.fori_loop(0, entries.shape[0] // 2, pair, 0)


def final_kernel(total, from_u, from_v, out):
    out[...] = (total[...] + from_u[...].astype(F32) + from_v[...].astype(F32)).astype(BF16)


def call(kernel, outs, places, scratch, us, *args, grant=VMEM_BYTES):
    spec = {"s": pl.BlockSpec(memory_space=pltpu.SMEM), "v": pl.BlockSpec(memory_space=pltpu.VMEM), "h": pl.BlockSpec(memory_space=pl.ANY), "d": pl.BlockSpec(memory_space=pltpu.HBM)}
    return pl.pallas_call(
        kernel,
        out_shape=outs,
        in_specs=[spec[p] for p in places],
        out_specs=jax.tree.map(lambda _: spec["v"], outs),
        scratch_shapes=scratch,
        compiler_params=pltpu.CompilerParams(vmem_limit_bytes=grant),
        cost_estimate=pl.CostEstimate(flops=int(us * 1e7), bytes_accessed=int(us * 3e4), transcendentals=0),
    )(*args)


def per_device(anomalies, innovations, obs_tile, pair_tiles, loc_bin):
    tiles, members, points = anomalies.shape
    slots = loc_bin.shape[0]
    size = lax.axis_size("tile")
    place = lax.axis_index("tile")
    to_u, to_v = routes(size, FROM_U), routes(size, FROM_V)
    send = lambda x, pairs: lax.ppermute(x, "tile", pairs)
    stay = lambda x: pltpu.with_memory_space_constraint(x, pltpu.HBM)
    swap = lambda x: lax.ppermute(x, "mem", [(0, 1), (1, 0)])

    sds = jax.ShapeDtypeStruct
    vm = pltpu.VMEM
    a_l = call(
        pack_kernel,
        sds((tiles * members + SLOT_ROWS, points), BF16),
        "hhh",
        [
            pltpu.SMEM((2, slots), jnp.int32),
            pltpu.SMEM((slots,), jnp.int32),
            pltpu.SemaphoreType.DMA((tiles + 2,)),
        ],
        1,
        stay(pair_tiles.T),
        stay(loc_bin),
        stay(anomalies),
    )
    a_v = send(a_l, to_v)
    a_u = send(a_l, to_u)
    a_t = swap(a_l)
    obs_tile, a_t = lax.optimization_barrier((obs_tile, a_t))
    weights = [vm((NBIN, WIDTH, points), F32), vm((points // WIDTH, points), F32)]
    forcing = call(
        forcing_kernel, sds(anomalies.shape, BF16), "sv", [vm(anomalies.shape, F32)], 1, obs_tile, stay(innovations)
    )
    g_v = send(forcing, to_v)
    g_u = send(forcing, to_u)
    other_list = jnp.where(place % 4 != 2, slot_codes(a_u, slots), slot_codes(a_v, slots))
    entries = entries_for(slot_codes(a_l, slots), other_list, place, tiles)
    a_ut = swap(a_u)
    a_vt = swap(a_v)

    groups = vm((2 * GROUPS, *a_l.shape), BF16)
    square = vm((points, points), BF16)
    far, inc_u, inc_v = call(
        early_kernel,
        (sds((slots, points, points), BF16), sds(anomalies.shape, F32), sds(anomalies.shape, F32)),
        "shhhhhhv",
        [groups, square, *weights, pltpu.SemaphoreType.DMA((2 * GROUPS,))],
        6,
        entries,
        a_l,
        a_t,
        a_u,
        a_ut,
        a_v,
        a_vt,
        forcing,
    )
    finish = lambda group, inc, g: call(
        functools.partial(far_kernel, group),
        sds(anomalies.shape, BF16),
        "svvv",
        [vm(anomalies.shape, F32)],
        1,
        entries,
        far,
        inc,
        g,
    )
    from_u = send(finish(1, inc_u, g_v), back(to_u))
    from_v = send(finish(2, inc_v, g_u), back(to_v))
    total = call(
        late_kernel,
        sds(anomalies.shape, F32),
        "shhhhhhvvv",
        [groups, vm((GROUPS * tiles, members, points), BF16), square, *weights, pltpu.SemaphoreType.DMA((2 * GROUPS,))],
        10,
        entries,
        a_l,
        a_t,
        a_u,
        a_ut,
        a_v,
        a_vt,
        forcing,
        g_u,
        g_v,
    )
    return call(final_kernel, sds(anomalies.shape, BF16), "vvv", [], 1, total, from_v, from_u)


def solution(mesh):
    return jax.shard_map(
        per_device,
        mesh=mesh,
        in_specs=(
            P("tile", "mem", None),
            P("tile", "mem", None),
            P("tile"),
            P("tile", None),
            P("tile"),
        ),
        out_specs=P("tile", "mem", None),
        check_vma=False,
    )
```

```python
import functools

import jax
import jax.numpy as jnp
from jax import lax
from jax.experimental import pallas as pl
from jax.experimental.pallas import tpu as pltpu
from jax.sharding import PartitionSpec as P

MEMBERS = 256
NBIN = 4
RADIUS = 4
WIDTH = 32
ROWS = 128
SLOT_ROWS = 16
F32 = jnp.float32
BF16 = jnp.bfloat16
VMEM_BYTES = 24 * 1024 * 1024
FULL_BYTES = 60 * 1024 * 1024

FROM_U = {0: 1, 1: 2, 2: 2}
FROM_V = {0: 2, 1: 4, 2: 1}


def routes(size, steps):
    return [(t + step, t) for t in range(size) for r, step in steps.items() if t % 4 == r and t + step < size]


def back(pairs):
    return [(b, a) for a, b in pairs]


def slot_codes(message, slots):
    rows = message.shape[0] - SLOT_ROWS
    parts = message[rows : rows + slots, :3].astype(jnp.int32)
    return parts[:, 0] + (parts[:, 1] << 8) + (parts[:, 2] << 16)


def entries_for(own, other, place, tiles):
    r = place % 4
    first, second = (own >> 8) & 255, own >> 16
    dist = second // tiles
    group = jnp.where(r == 0, dist, jnp.where(r == 2, 3 - dist, jnp.where((r == 1) & (dist == 2), 1, -1)))
    group = jnp.where(dist == 0, 0, group)
    entry = (own & 65535) + ((second % tiles + tiles * group) << 16)
    near = jnp.where((own > 0) & (group >= 0), entry, 0)
    first, second = (other >> 8) & 255, other >> 16
    dist = second // tiles
    second = second % tiles
    turned = r == 2
    entry = (other & 255) + jnp.where(turned, 2 * NBIN, 0)
    entry = entry + (jnp.where(turned, second, first) << 8) + (jnp.where(turned, first, second) << 16)
    far = jnp.where((other > 0) & (r != 3) & (dist == jnp.where(r == 1, 2, 1)), entry, 0)
    return jnp.concatenate([near, far])


def decode(entry):
    return lax.shift_right_logical(entry, 1) & 127, lax.shift_right_logical(entry, 8) & 255, lax.shift_right_logical(entry, 16)


def fill_weights(along, across, points):
    q = lax.broadcasted_iota(jnp.int32, (WIDTH, points), 1) % WIDTH
    p = lax.broadcasted_iota(jnp.int32, (WIDTH, points), 0)
    gap = (q - p).astype(F32)
    for k in range(along.shape[0]):
        shift = (gap if k < NBIN else -gap) + 0.5 * RADIUS * (k % NBIN)
        along[k] = jnp.exp(-(shift * shift) / (2.0 * RADIUS * RADIUS))
    levels = points // WIDTH
    row = lax.broadcasted_iota(jnp.int32, (levels, points), 1) // WIDTH
    level = lax.broadcasted_iota(jnp.int32, (levels, points), 0)
    gap = (row - level).astype(F32)
    across[...] = jnp.exp(-(gap * gap) / (2.0 * RADIUS * RADIUS)) / (MEMBERS - 1)


def both(halves, tile, cols):
    rows = pl.ds(pl.multiple_of(tile * ROWS, ROWS), ROWS)
    return jnp.concatenate([half[rows, cols] for half in halves], axis=0)


def covariance(left, right, first, second, weight, across, out):
    points = out.shape[1]
    values = both(right, second, slice(None))
    for p0 in range(0, points, ROWS):
        cross = lax.dot_general(
            both(left, first, slice(p0, p0 + ROWS)), values, (((0,), (0,)), ((), ())), preferred_element_type=F32
        )
        for row in range(0, ROWS, WIDTH):
            level = (p0 + row) // WIDTH
            part = cross[row : row + WIDTH] * (weight * across[pl.ds(level, 1), :])
            out[pl.ds(p0 + row, WIDTH), :] = part.astype(BF16)


def to_first(g, c):
    return lax.dot_general(g, c, (((1,), (1,)), ((), ())), preferred_element_type=F32)


def to_second(g, c):
    return lax.dot_general(g, c, (((1,), (0,)), ((), ())), preferred_element_type=F32)


def pack_kernel(pairs, bins, anomalies, out, pairs_s, bins_s, sems):
    tiles, members = anomalies.shape[0], anomalies.shape[1]
    slots = bins.shape[0]
    copies = [pltpu.make_async_copy(pairs, pairs_s, sems.at[tiles]), pltpu.make_async_copy(bins, bins_s, sems.at[tiles + 1])]
    for t in range(tiles):
        copies.append(pltpu.make_async_copy(anomalies.at[t], out.at[pl.ds(t * members, members), :], sems.at[t]))
    for copy in copies:
        copy.start()
    copies[0].wait()
    copies[1].wait()
    row = lax.broadcasted_iota(jnp.int32, (SLOT_ROWS, 128), 0)
    lane = lax.broadcasted_iota(jnp.int32, (SLOT_ROWS, 128), 1)
    value = jnp.zeros(lane.shape, jnp.int32)
    for k in range(slots):
        first = lax.rem(pairs_s[0, k], tiles)
        second = pairs_s[1, k] - pairs_s[0, k] + first
        parts = jnp.where(lane == 0, 1 + 2 * bins_s[k], jnp.where(lane == 1, first, jnp.where(lane == 2, second, 0)))
        value = jnp.where((row == k) & (bins_s[k] < NBIN), parts, value)
    out[pl.ds(tiles * members, SLOT_ROWS), :] = jnp.zeros((SLOT_ROWS, out.shape[1]), BF16)
    out[pl.ds(tiles * members, SLOT_ROWS), pl.ds(0, 128)] = value.astype(F32).astype(BF16)
    for copy in copies[2:]:
        copy.wait()


def forcing_kernel(obs, innov, out, total):
    tiles = out.shape[0]
    total[...] = jnp.zeros_like(total)

    def step(o, carry):
        t = lax.rem(obs[o], tiles)
        total[t] = total[t] + innov[o].astype(F32)
        return carry

    lax.fori_loop(0, innov.shape[0], step, 0)
    out[...] = total[...].astype(BF16)


def add_near(group, entries, left, right, g, inc, c, along, across):
    tiles = g.shape[0]

    def pair(k, carry):
        entry = entries[k]
        bins, first, second = decode(entry)
        here = second - group * tiles

        @pl.when((entry > 0) & (here >= 0) & (here < tiles))
        def _():
            covariance(left, right, first, here, along[bins], across, c)
            inc[here] = inc[here] + to_second(g[first], c[...])

        return carry

    lax.fori_loop(0, entries.shape[0] // 2, pair, 0)


def early_kernel(entries, lm, lt, um, ut, vm, vt, g, far, inc_u, inc_v, c, along, across):
    fill_weights(along, across, c.shape[1])
    inc_u[...] = jnp.zeros_like(inc_u)
    inc_v[...] = jnp.zeros_like(inc_v)
    add_near(1, entries, (lm, lt), (um, ut), g, inc_u, c, along, across)
    add_near(2, entries, (lm, lt), (vm, vt), g, inc_v, c, along, across)
    slots = entries.shape[0] // 2

    def pair(k, carry):
        entry = entries[slots + k]
        bins, first, second = decode(entry)

        @pl.when(entry > 0)
        def _():
            covariance((um, ut), (vm, vt), first, second, along[bins], across, far.at[k])

        return carry

    lax.fori_loop(0, slots, pair, 0)


def far_kernel(group, entries, far, inc, g, out, total):
    slots = entries.shape[0] // 2
    total[...] = inc[...]

    def pair(k, carry):
        entry = entries[slots + k]
        _, first, second = decode(entry)

        @pl.when(entry > 0)
        def _():
            if group == 1:
                total[first] = total[first] + to_first(g[second], far[k])
            else:
                total[second] = total[second] + to_second(g[first], far[k])

        return carry

    lax.fori_loop(0, slots, pair, 0)
    out[...] = total[...].astype(BF16)


def late_kernel(entries, lm, lt, um, ut, vm, vt, g_l, g_u, g_v, out, c, along, across):
    tiles, members, points = g_l.shape
    fill_weights(along, across, points)

    def own(t, carry):
        covariance((lm, lt), (lm, lt), t, t, along[0], across, c)
        rows = pl.ds(pl.multiple_of(t * members, members), members)
        out[t] = lm[rows, :].astype(F32) + to_first(g_l[t], c[...])
        return carry

    lax.fori_loop(0, tiles, own, 0)

    def pair(k, carry):
        entry = entries[k]
        bins, first, second = decode(entry)

        for group, (right, g) in enumerate((((lm, lt), g_l), ((um, ut), g_u), ((vm, vt), g_v))):
            here = second - group * tiles

            @pl.when((entry > 0) & (here >= 0) & (here < tiles))
            def _():
                covariance((lm, lt), right, first, here, along[bins], across, c)
                out[first] = out[first] + to_first(g[here], c[...])
                if group == 0:
                    out[here] = out[here] + to_second(g_l[first], c[...])

        return carry

    lax.fori_loop(0, entries.shape[0] // 2, pair, 0)


def final_kernel(total, from_u, from_v, out, done, sems):
    copies = []
    for t in range(total.shape[0]):
        done[t] = (total[t] + from_u[t].astype(F32) + from_v[t].astype(F32)).astype(BF16)
        copies.append(pltpu.make_async_copy(done.at[t], out.at[t], sems.at[t]))
        copies[-1].start()
    for copy in copies:
        copy.wait()


def call(kernel, outs, places, scratch, us, *args, grant=VMEM_BYTES, to="v"):
    spec = {"s": pl.BlockSpec(memory_space=pltpu.SMEM), "v": pl.BlockSpec(memory_space=pltpu.VMEM), "h": pl.BlockSpec(memory_space=pl.ANY), "d": pl.BlockSpec(memory_space=pltpu.HBM)}
    return pl.pallas_call(
        kernel,
        out_shape=outs,
        in_specs=[spec[p] for p in places],
        out_specs=jax.tree.map(lambda _: spec[to], outs),
        scratch_shapes=scratch,
        compiler_params=pltpu.CompilerParams(vmem_limit_bytes=grant),
        cost_estimate=pl.CostEstimate(flops=int(us * 1e7), bytes_accessed=int(us * 3e4), transcendentals=0),
    )(*args)


def per_device(anomalies, innovations, obs_tile, pair_tiles, loc_bin):
    tiles, members, points = anomalies.shape
    slots = loc_bin.shape[0]
    size = lax.axis_size("tile")
    place = lax.axis_index("tile")
    to_u, to_v = routes(size, FROM_U), routes(size, FROM_V)
    send = lambda x, pairs: lax.ppermute(x, "tile", pairs)
    stay = lambda x: pltpu.with_memory_space_constraint(x, pltpu.HBM)
    swap = lambda x: lax.ppermute(x, "mem", [(0, 1), (1, 0)])

    sds = jax.ShapeDtypeStruct
    vm = pltpu.VMEM
    a_l = call(
        pack_kernel,
        sds((tiles * members + SLOT_ROWS, points), BF16),
        "hhh",
        [
            pltpu.SMEM((2, slots), jnp.int32),
            pltpu.SMEM((slots,), jnp.int32),
            pltpu.SemaphoreType.DMA((tiles + 2,)),
        ],
        1,
        stay(pair_tiles.T),
        stay(loc_bin),
        stay(anomalies),
    )
    a_v = send(a_l, to_v)
    a_u = send(a_l, to_u)
    a_t = swap(a_l)
    obs_tile, a_t = lax.optimization_barrier((obs_tile, a_t))
    forcing = call(
        forcing_kernel, sds(anomalies.shape, BF16), "sv", [vm(anomalies.shape, F32)], 1, obs_tile, stay(innovations)
    )
    g_v = send(forcing, to_v)
    g_u = send(forcing, to_u)
    other_list = jnp.where(place % 4 != 2, slot_codes(a_u, slots), slot_codes(a_v, slots))
    entries = entries_for(slot_codes(a_l, slots), other_list, place, tiles)
    square = vm((points, points), BF16)
    across = vm((points // WIDTH, points), F32)
    weights = [square, vm((NBIN, WIDTH, points), F32), across]
    weights_far = [square, vm((2 * NBIN, WIDTH, points), F32), across]

    a_vt = swap(a_v)
    a_ut = swap(a_u)
    far, inc_u, inc_v = call(
        early_kernel,
        (sds((slots, points, points), BF16), sds(anomalies.shape, F32), sds(anomalies.shape, F32)),
        "svvvvvvv",
        weights_far,
        4,
        entries,
        a_l,
        a_t,
        a_u,
        a_ut,
        a_v,
        a_vt,
        forcing,
    )
    finish = lambda group, inc, g: call(
        functools.partial(far_kernel, group),
        sds(anomalies.shape, BF16),
        "svvv",
        [vm(anomalies.shape, F32)],
        1,
        entries,
        far,
        inc,
        g,
    )
    from_u = send(finish(1, inc_u, g_v), back(to_u))
    from_v = send(finish(2, inc_v, g_u), back(to_v))
    total = call(
        late_kernel,
        sds(anomalies.shape, F32),
        "svvvvvvvvv",
        weights,
        10,
        entries,
        a_l,
        a_t,
        a_u,
        a_ut,
        a_v,
        a_vt,
        forcing,
        g_u,
        g_v,
    )
    return call(
        final_kernel,
        sds(anomalies.shape, BF16),
        "vvv",
        [vm(anomalies.shape, BF16), pltpu.SemaphoreType.DMA((tiles,))],
        1,
        total,
        from_v,
        from_u,
        to="h",
    )


def solution(mesh):
    return jax.shard_map(
        per_device,
        mesh=mesh,
        in_specs=(
            P("tile", "mem", None),
            P("tile", "mem", None),
            P("tile"),
            P("tile", None),
            P("tile"),
        ),
        out_specs=P("tile", "mem", None),
        check_vma=False,
    )
```

```python
import functools

import jax
import jax.numpy as jnp
from jax import lax
from jax.experimental import pallas as pl
from jax.experimental.pallas import tpu as pltpu
from jax.sharding import PartitionSpec as P

MEMBERS = 256
NBIN = 4
RADIUS = 4
WIDTH = 32
ROWS = 128
SLOT_ROWS = 16
F32 = jnp.float32
BF16 = jnp.bfloat16
VMEM_BYTES = 24 * 1024 * 1024
FULL_BYTES = 60 * 1024 * 1024

FROM_U = {0: 1, 1: 2, 2: 2}
FROM_V = {0: 2, 1: 4, 2: 1}


def routes(size, steps):
    return [(t + step, t) for t in range(size) for r, step in steps.items() if t % 4 == r and t + step < size]


def back(pairs):
    return [(b, a) for a, b in pairs]


def slot_codes(message, slots):
    rows = message.shape[0] - SLOT_ROWS
    parts = message[rows : rows + slots, :3].astype(jnp.int32)
    return parts[:, 0] + (parts[:, 1] << 8) + (parts[:, 2] << 16)


def entries_for(own, other, place, tiles):
    r = place % 4
    first, second = (own >> 8) & 255, own >> 16
    dist = second // tiles
    group = jnp.where(r == 0, dist, jnp.where(r == 2, 3 - dist, jnp.where((r == 1) & (dist == 2), 1, -1)))
    group = jnp.where(dist == 0, 0, group)
    entry = (own & 65535) + ((second % tiles + tiles * group) << 16)
    near = jnp.where((own > 0) & (group >= 0), entry, 0)
    first, second = (other >> 8) & 255, other >> 16
    dist = second // tiles
    second = second % tiles
    turned = r == 2
    entry = (other & 255) + jnp.where(turned, 2 * NBIN, 0)
    entry = entry + (jnp.where(turned, second, first) << 8) + (jnp.where(turned, first, second) << 16)
    far = jnp.where((other > 0) & (r != 3) & (dist == jnp.where(r == 1, 2, 1)), entry, 0)
    return near[None], far[None]


def decode(entry):
    return lax.shift_right_logical(entry, 1) & 127, lax.shift_right_logical(entry, 8) & 255, lax.shift_right_logical(entry, 16)


def read_slots(entries, ints):
    row = entries[...]
    lane = lax.broadcasted_iota(jnp.int32, row.shape, 1)
    for k in range(row.shape[1]):
        ints[k] = jnp.max(jnp.where(lane == k, row, 0))


def fill_weights(along, across, points):
    q = lax.broadcasted_iota(jnp.int32, (WIDTH, points), 1) % WIDTH
    p = lax.broadcasted_iota(jnp.int32, (WIDTH, points), 0)
    gap = (q - p).astype(F32)
    for k in range(along.shape[0]):
        shift = (gap if k < NBIN else -gap) + 0.5 * RADIUS * (k % NBIN)
        along[k] = jnp.exp(-(shift * shift) / (2.0 * RADIUS * RADIUS))
    levels = points // WIDTH
    row = lax.broadcasted_iota(jnp.int32, (levels, points), 1) // WIDTH
    level = lax.broadcasted_iota(jnp.int32, (levels, points), 0)
    gap = (row - level).astype(F32)
    across[...] = jnp.exp(-(gap * gap) / (2.0 * RADIUS * RADIUS)) / (MEMBERS - 1)


def both(halves, tile, cols):
    rows = pl.ds(pl.multiple_of(tile * ROWS, ROWS), ROWS)
    return jnp.concatenate([half[rows, cols] for half in halves], axis=0)


def covariance(left, right, first, second, weight, across, out):
    points = out.shape[1]
    values = both(right, second, slice(None))
    for p0 in range(0, points, ROWS):
        cross = lax.dot_general(
            both(left, first, slice(p0, p0 + ROWS)), values, (((0,), (0,)), ((), ())), preferred_element_type=F32
        )
        for row in range(0, ROWS, WIDTH):
            level = (p0 + row) // WIDTH
            part = cross[row : row + WIDTH] * (weight * across[pl.ds(level, 1), :])
            out[pl.ds(p0 + row, WIDTH), :] = part.astype(BF16)


def to_first(g, c):
    return lax.dot_general(g, c, (((1,), (1,)), ((), ())), preferred_element_type=F32)


def to_second(g, c):
    return lax.dot_general(g, c, (((1,), (0,)), ((), ())), preferred_element_type=F32)


def pack_kernel(pairs, bins, anomalies, out, pairs_s, bins_s, sems):
    tiles, members = anomalies.shape[0], anomalies.shape[1]
    slots = bins.shape[0]
    copies = [pltpu.make_async_copy(pairs, pairs_s, sems.at[tiles]), pltpu.make_async_copy(bins, bins_s, sems.at[tiles + 1])]
    for t in range(tiles):
        copies.append(pltpu.make_async_copy(anomalies.at[t], out.at[pl.ds(t * members, members), :], sems.at[t]))
    for copy in copies:
        copy.start()
    copies[0].wait()
    copies[1].wait()
    row = lax.broadcasted_iota(jnp.int32, (SLOT_ROWS, 128), 0)
    lane = lax.broadcasted_iota(jnp.int32, (SLOT_ROWS, 128), 1)
    value = jnp.zeros(lane.shape, jnp.int32)
    for k in range(slots):
        first = lax.rem(pairs_s[0, k], tiles)
        second = pairs_s[1, k] - pairs_s[0, k] + first
        parts = jnp.where(lane == 0, 1 + 2 * bins_s[k], jnp.where(lane == 1, first, jnp.where(lane == 2, second, 0)))
        value = jnp.where((row == k) & (bins_s[k] < NBIN), parts, value)
    out[pl.ds(tiles * members, SLOT_ROWS), :] = jnp.zeros((SLOT_ROWS, out.shape[1]), BF16)
    out[pl.ds(tiles * members, SLOT_ROWS), pl.ds(0, 128)] = value.astype(F32).astype(BF16)
    for copy in copies[2:]:
        copy.wait()


def forcing_kernel(obs, innov, out, total):
    tiles = out.shape[0]
    total[...] = jnp.zeros_like(total)

    def step(o, carry):
        t = lax.rem(obs[o], tiles)
        total[t] = total[t] + innov[o].astype(F32)
        return carry

    lax.fori_loop(0, innov.shape[0], step, 0)
    out[...] = total[...].astype(BF16)


def add_near(group, entries, left, right, g, inc, c, along, across):
    tiles = g.shape[0]

    def pair(k, carry):
        entry = entries[k]
        bins, first, second = decode(entry)
        here = second - group * tiles

        @pl.when((entry > 0) & (here >= 0) & (here < tiles))
        def _():
            covariance(left, right, first, here, along[bins], across, c)
            inc[here] = inc[here] + to_second(g[first], c[...])

        return carry

    lax.fori_loop(0, entries.shape[0], pair, 0)


def early_kernel(near, far_slots, lm, lt, um, ut, vm, vt, g, far, inc_u, inc_v, c, along, across, near_s, far_s):
    read_slots(near, near_s)
    read_slots(far_slots, far_s)
    fill_weights(along, across, c.shape[1])
    inc_u[...] = jnp.zeros_like(inc_u)
    inc_v[...] = jnp.zeros_like(inc_v)
    add_near(1, near_s, (lm, lt), (um, ut), g, inc_u, c, along, across)
    add_near(2, near_s, (lm, lt), (vm, vt), g, inc_v, c, along, across)
    slots = far.shape[0]

    def pair(k, carry):
        entry = far_s[k]
        bins, first, second = decode(entry)

        @pl.when(entry > 0)
        def _():
            covariance((um, ut), (vm, vt), first, second, along[bins], across, far.at[k])

        return carry

    lax.fori_loop(0, slots, pair, 0)


def far_kernel(group, far_slots, far, inc, g, out, total, far_s):
    read_slots(far_slots, far_s)
    total[...] = inc[...]

    def pair(k, carry):
        entry = far_s[k]
        _, first, second = decode(entry)

        @pl.when(entry > 0)
        def _():
            if group == 1:
                total[first] = total[first] + to_first(g[second], far[k])
            else:
                total[second] = total[second] + to_second(g[first], far[k])

        return carry

    lax.fori_loop(0, far.shape[0], pair, 0)
    out[...] = total[...].astype(BF16)


def late_kernel(near, lm, lt, um, ut, vm, vt, g_l, g_u, g_v, out, c, along, across, near_s):
    read_slots(near, near_s)
    tiles, members, points = g_l.shape
    fill_weights(along, across, points)

    def own(t, carry):
        covariance((lm, lt), (lm, lt), t, t, along[0], across, c)
        rows = pl.ds(pl.multiple_of(t * members, members), members)
        out[t] = lm[rows, :].astype(F32) + to_first(g_l[t], c[...])
        return carry

    lax.fori_loop(0, tiles, own, 0)

    def pair(k, carry):
        entry = near_s[k]
        bins, first, second = decode(entry)

        for group, (right, g) in enumerate((((lm, lt), g_l), ((um, ut), g_u), ((vm, vt), g_v))):
            here = second - group * tiles

            @pl.when((entry > 0) & (here >= 0) & (here < tiles))
            def _():
                covariance((lm, lt), right, first, here, along[bins], across, c)
                out[first] = out[first] + to_first(g[here], c[...])
                if group == 0:
                    out[here] = out[here] + to_second(g_l[first], c[...])

        return carry

    lax.fori_loop(0, near.shape[1], pair, 0)


def final_kernel(total, from_u, from_v, out, done, sems):
    copies = []
    for t in range(total.shape[0]):
        done[t] = (total[t] + from_u[t].astype(F32) + from_v[t].astype(F32)).astype(BF16)
        copies.append(pltpu.make_async_copy(done.at[t], out.at[t], sems.at[t]))
        copies[-1].start()
    for copy in copies:
        copy.wait()


def call(kernel, outs, places, scratch, us, *args, grant=VMEM_BYTES, to="v"):
    spec = {"s": pl.BlockSpec(memory_space=pltpu.SMEM), "v": pl.BlockSpec(memory_space=pltpu.VMEM), "h": pl.BlockSpec(memory_space=pl.ANY), "d": pl.BlockSpec(memory_space=pltpu.HBM)}
    return pl.pallas_call(
        kernel,
        out_shape=outs,
        in_specs=[spec[p] for p in places],
        out_specs=jax.tree.map(lambda _: spec[to], outs),
        scratch_shapes=scratch,
        compiler_params=pltpu.CompilerParams(vmem_limit_bytes=grant),
        cost_estimate=pl.CostEstimate(flops=int(us * 1e7), bytes_accessed=int(us * 3e4), transcendentals=0),
    )(*args)


def per_device(anomalies, innovations, obs_tile, pair_tiles, loc_bin):
    tiles, members, points = anomalies.shape
    slots = loc_bin.shape[0]
    size = lax.axis_size("tile")
    place = lax.axis_index("tile")
    to_u, to_v = routes(size, FROM_U), routes(size, FROM_V)
    send = lambda x, pairs: lax.ppermute(x, "tile", pairs)
    stay = lambda x: pltpu.with_memory_space_constraint(x, pltpu.HBM)
    swap = lambda x: lax.ppermute(x, "mem", [(0, 1), (1, 0)])

    sds = jax.ShapeDtypeStruct
    vm = pltpu.VMEM
    a_l = call(
        pack_kernel,
        sds((tiles * members + SLOT_ROWS, points), BF16),
        "hhh",
        [
            pltpu.SMEM((2, slots), jnp.int32),
            pltpu.SMEM((slots,), jnp.int32),
            pltpu.SemaphoreType.DMA((tiles + 2,)),
        ],
        1,
        stay(pair_tiles.T),
        stay(loc_bin),
        stay(anomalies),
    )
    a_v = send(a_l, to_v)
    a_u = send(a_l, to_u)
    a_t = swap(a_l)
    obs_tile, a_t = lax.optimization_barrier((obs_tile, a_t))
    forcing = call(
        forcing_kernel, sds(anomalies.shape, BF16), "sv", [vm(anomalies.shape, F32)], 1, obs_tile, stay(innovations)
    )
    g_v = send(forcing, to_v)
    g_u = send(forcing, to_u)
    other_list = jnp.where(place % 4 != 2, slot_codes(a_u, slots), slot_codes(a_v, slots))
    near, far_slots = entries_for(slot_codes(a_l, slots), other_list, place, tiles)
    square = vm((points, points), BF16)
    across = vm((points // WIDTH, points), F32)
    weights = [square, vm((NBIN, WIDTH, points), F32), across]
    weights_far = [square, vm((2 * NBIN, WIDTH, points), F32), across]
    ints = pltpu.SMEM((slots,), jnp.int32)

    a_vt = swap(a_v)
    a_ut = swap(a_u)
    far, inc_u, inc_v = call(
        early_kernel,
        (sds((slots, points, points), BF16), sds(anomalies.shape, F32), sds(anomalies.shape, F32)),
        "vvvvvvvvv",
        [*weights_far, ints, ints],
        4,
        near,
        far_slots,
        a_l,
        a_t,
        a_u,
        a_ut,
        a_v,
        a_vt,
        forcing,
    )
    finish = lambda group, inc, g: call(
        functools.partial(far_kernel, group),
        sds(anomalies.shape, BF16),
        "vvvv",
        [vm(anomalies.shape, F32), ints],
        1,
        far_slots,
        far,
        inc,
        g,
    )
    from_u = send(finish(1, inc_u, g_v), back(to_u))
    from_v = send(finish(2, inc_v, g_u), back(to_v))
    total = call(
        late_kernel,
        sds(anomalies.shape, F32),
        "vvvvvvvvvv",
        [*weights, ints],
        10,
        near,
        a_l,
        a_t,
        a_u,
        a_ut,
        a_v,
        a_vt,
        forcing,
        g_u,
        g_v,
    )
    return call(
        final_kernel,
        sds(anomalies.shape, BF16),
        "vvv",
        [vm(anomalies.shape, BF16), pltpu.SemaphoreType.DMA((tiles,))],
        1,
        total,
        from_v,
        from_u,
        to="h",
    )


def solution(mesh):
    return jax.shard_map(
        per_device,
        mesh=mesh,
        in_specs=(
            P("tile", "mem", None),
            P("tile", "mem", None),
            P("tile"),
            P("tile", None),
            P("tile"),
        ),
        out_specs=P("tile", "mem", None),
        check_vma=False,
    )
```

```python
import functools

import jax
import jax.numpy as jnp
from jax import lax
from jax.experimental import pallas as pl
from jax.experimental.pallas import tpu as pltpu
from jax.sharding import PartitionSpec as P

MEMBERS = 256
NBIN = 4
RADIUS = 4
WIDTH = 32
ROWS = 128
SLOT_ROWS = 16
F32 = jnp.float32
BF16 = jnp.bfloat16
VMEM_BYTES = 24 * 1024 * 1024
FULL_BYTES = 60 * 1024 * 1024

FROM_U = {0: 1, 1: 2, 2: 2}
FROM_V = {0: 2, 1: 4, 2: 1}


def routes(size, steps):
    return [(t + step, t) for t in range(size) for r, step in steps.items() if t % 4 == r and t + step < size]


def back(pairs):
    return [(b, a) for a, b in pairs]


def slot_codes(message, slots):
    rows = message.shape[0] - SLOT_ROWS
    parts = message[rows : rows + slots, :3].astype(jnp.int32)
    return parts[:, 0] + (parts[:, 1] << 8) + (parts[:, 2] << 16)


def entries_for(own, other, place, tiles):
    r = place % 4
    first, second = (own >> 8) & 255, own >> 16
    dist = second // tiles
    group = jnp.where(r == 0, dist, jnp.where(r == 2, 3 - dist, jnp.where((r == 1) & (dist == 2), 1, -1)))
    group = jnp.where(dist == 0, 0, group)
    entry = (own & 65535) + ((second % tiles + tiles * group) << 16)
    near = jnp.where((own > 0) & (group >= 0), entry, 0)
    first, second = (other >> 8) & 255, other >> 16
    dist = second // tiles
    second = second % tiles
    turned = r == 2
    entry = (other & 255) + jnp.where(turned, 2 * NBIN, 0)
    entry = entry + (jnp.where(turned, second, first) << 8) + (jnp.where(turned, first, second) << 16)
    far = jnp.where((other > 0) & (r != 3) & (dist == jnp.where(r == 1, 2, 1)), entry, 0)
    return near[None], far[None]


def decode(entry):
    return lax.shift_right_logical(entry, 1) & 127, lax.shift_right_logical(entry, 8) & 255, lax.shift_right_logical(entry, 16)


def read_slots(entries, ints):
    row = entries[...]
    lane = lax.broadcasted_iota(jnp.int32, row.shape, 1)
    for k in range(row.shape[1]):
        ints[k] = jnp.max(jnp.where(lane == k, row, 0))


def fill_weights(along, across, points):
    q = lax.broadcasted_iota(jnp.int32, (WIDTH, points), 1) % WIDTH
    p = lax.broadcasted_iota(jnp.int32, (WIDTH, points), 0)
    gap = (q - p).astype(F32)
    for k in range(along.shape[0]):
        shift = (gap if k < NBIN else -gap) + 0.5 * RADIUS * (k % NBIN)
        along[k] = jnp.exp(-(shift * shift) / (2.0 * RADIUS * RADIUS))
    levels = points // WIDTH
    row = lax.broadcasted_iota(jnp.int32, (levels, points), 1) // WIDTH
    level = lax.broadcasted_iota(jnp.int32, (levels, points), 0)
    gap = (row - level).astype(F32)
    across[...] = jnp.exp(-(gap * gap) / (2.0 * RADIUS * RADIUS)) / (MEMBERS - 1)


def both(halves, tile, cols):
    rows = pl.ds(pl.multiple_of(tile * ROWS, ROWS), ROWS)
    return jnp.concatenate([half[rows, cols] for half in halves], axis=0)


def covariance(left, right, first, second, weight, across, out):
    points = out.shape[1]
    values = both(right, second, slice(None))
    for p0 in range(0, points, ROWS):
        cross = lax.dot_general(
            both(left, first, slice(p0, p0 + ROWS)), values, (((0,), (0,)), ((), ())), preferred_element_type=F32
        )
        for row in range(0, ROWS, WIDTH):
            level = (p0 + row) // WIDTH
            part = cross[row : row + WIDTH] * (weight * across[pl.ds(level, 1), :])
            out[pl.ds(p0 + row, WIDTH), :] = part.astype(BF16)


def to_first(g, c):
    return lax.dot_general(g, c, (((1,), (1,)), ((), ())), preferred_element_type=F32)


def to_second(g, c):
    return lax.dot_general(g, c, (((1,), (0,)), ((), ())), preferred_element_type=F32)


def pack_kernel(pairs, bins, anomalies, out, pairs_s, bins_s, sems):
    tiles, members = anomalies.shape[0], anomalies.shape[1]
    slots = bins.shape[0]
    copies = [pltpu.make_async_copy(pairs, pairs_s, sems.at[tiles]), pltpu.make_async_copy(bins, bins_s, sems.at[tiles + 1])]
    for t in range(tiles):
        copies.append(pltpu.make_async_copy(anomalies.at[t], out.at[pl.ds(t * members, members), :], sems.at[t]))
    for copy in copies:
        copy.start()
    copies[0].wait()
    copies[1].wait()
    row = lax.broadcasted_iota(jnp.int32, (SLOT_ROWS, 128), 0)
    lane = lax.broadcasted_iota(jnp.int32, (SLOT_ROWS, 128), 1)
    value = jnp.zeros(lane.shape, jnp.int32)
    for k in range(slots):
        first = lax.rem(pairs_s[0, k], tiles)
        second = pairs_s[1, k] - pairs_s[0, k] + first
        parts = jnp.where(lane == 0, 1 + 2 * bins_s[k], jnp.where(lane == 1, first, jnp.where(lane == 2, second, 0)))
        value = jnp.where((row == k) & (bins_s[k] < NBIN), parts, value)
    out[pl.ds(tiles * members, SLOT_ROWS), :] = jnp.zeros((SLOT_ROWS, out.shape[1]), BF16)
    out[pl.ds(tiles * members, SLOT_ROWS), pl.ds(0, 128)] = value.astype(F32).astype(BF16)
    for copy in copies[2:]:
        copy.wait()


def forcing_kernel(obs, innov, out, total):
    tiles = out.shape[0]
    total[...] = jnp.zeros_like(total)

    def step(o, carry):
        t = lax.rem(obs[o], tiles)
        total[t] = total[t] + innov[o].astype(F32)
        return carry

    lax.fori_loop(0, innov.shape[0], step, 0)
    out[...] = total[...].astype(BF16)


def compact(ints, wanted, kept):
    count = jnp.int32(0)
    for k in range(ints.shape[0]):
        kept[count] = ints[k]
        count = count + wanted(ints[k]).astype(jnp.int32)
    return count


def in_twos(count, step):
    def two(k, carry):
        step([2 * k, 2 * k + 1])
        return carry

    lax.fori_loop(0, lax.div(count, 2), two, 0)

    @pl.when(lax.rem(count, 2) == 1)
    def _():
        step([count - 1])


def add_near(group, ints, kept, left, right, g, inc, c, along, across):
    tiles = g.shape[0]

    def wanted(entry):
        _, _, second = decode(entry)
        return (entry > 0) & (second >= group * tiles) & (second < (group + 1) * tiles)

    def step(indices):
        pairs = [decode(kept[k]) for k in indices]
        for q, (bins, first, second) in enumerate(pairs):
            covariance(left, right, first, second - group * tiles, along[bins], across, c.at[q])
        parts = [to_second(g[first], c[q]) for q, (_, first, _) in enumerate(pairs)]
        for part, (_, _, second) in zip(parts, pairs):
            here = second - group * tiles
            inc[here] = inc[here] + part

    in_twos(compact(ints, wanted, kept), step)


def early_kernel(near, far_slots, lm, lt, um, ut, vm, vt, g, far, inc_u, inc_v, c, along, across, ints, kept):
    points = c.shape[1]
    read_slots(near, ints)
    fill_weights(along, across, points)
    inc_u[...] = jnp.zeros_like(inc_u)
    inc_v[...] = jnp.zeros_like(inc_v)
    add_near(1, ints, kept, (lm, lt), (um, ut), g, inc_u, c, along, across)
    add_near(2, ints, kept, (lm, lt), (vm, vt), g, inc_v, c, along, across)
    read_slots(far_slots, ints)

    def step(indices):
        for k in indices:
            bins, first, second = decode(kept[k])
            covariance((um, ut), (vm, vt), first, second, along[bins], across, far.at[k])

    in_twos(compact(ints, lambda entry: entry > 0, kept), step)


def far_kernel(group, far_slots, far, inc, g, out, total, ints, kept):
    read_slots(far_slots, ints)
    total[...] = inc[...]

    def step(indices):
        pairs = [decode(kept[k])[1:] for k in indices]
        if group == 1:
            parts = [to_first(g[second], far[k]) for k, (_, second) in zip(indices, pairs)]
            places = [first for first, _ in pairs]
        else:
            parts = [to_second(g[first], far[k]) for k, (first, _) in zip(indices, pairs)]
            places = [second for _, second in pairs]
        for part, here in zip(parts, places):
            total[here] = total[here] + part

    in_twos(compact(ints, lambda entry: entry > 0, kept), step)
    out[...] = total[...].astype(BF16)


def late_kernel(near, lm, lt, um, ut, vm, vt, g_l, g_u, g_v, out, c, along, across, near_s):
    read_slots(near, near_s)
    tiles, members, points = g_l.shape
    fill_weights(along, across, points)

    def own(t, carry):
        covariance((lm, lt), (lm, lt), t, t, along[0], across, c)
        rows = pl.ds(pl.multiple_of(t * members, members), members)
        out[t] = lm[rows, :].astype(F32) + to_first(g_l[t], c[...])
        return carry

    lax.fori_loop(0, tiles, own, 0)

    def pair(k, carry):
        entry = near_s[k]
        bins, first, second = decode(entry)

        for group, (right, g) in enumerate((((lm, lt), g_l), ((um, ut), g_u), ((vm, vt), g_v))):
            here = second - group * tiles

            @pl.when((entry > 0) & (here >= 0) & (here < tiles))
            def _():
                covariance((lm, lt), right, first, here, along[bins], across, c)
                out[first] = out[first] + to_first(g[here], c[...])
                if group == 0:
                    out[here] = out[here] + to_second(g_l[first], c[...])

        return carry

    lax.fori_loop(0, near.shape[1], pair, 0)


def final_kernel(total, from_u, from_v, out, done, sems):
    copies = []
    for t in range(total.shape[0]):
        done[t] = (total[t] + from_u[t].astype(F32) + from_v[t].astype(F32)).astype(BF16)
        copies.append(pltpu.make_async_copy(done.at[t], out.at[t], sems.at[t]))
        copies[-1].start()
    for copy in copies:
        copy.wait()


def call(kernel, outs, places, scratch, us, *args, grant=VMEM_BYTES, to="v"):
    spec = {"s": pl.BlockSpec(memory_space=pltpu.SMEM), "v": pl.BlockSpec(memory_space=pltpu.VMEM), "h": pl.BlockSpec(memory_space=pl.ANY), "d": pl.BlockSpec(memory_space=pltpu.HBM)}
    return pl.pallas_call(
        kernel,
        out_shape=outs,
        in_specs=[spec[p] for p in places],
        out_specs=jax.tree.map(lambda _: spec[to], outs),
        scratch_shapes=scratch,
        compiler_params=pltpu.CompilerParams(vmem_limit_bytes=grant),
        cost_estimate=pl.CostEstimate(flops=int(us * 1e7), bytes_accessed=int(us * 3e4), transcendentals=0),
    )(*args)


def per_device(anomalies, innovations, obs_tile, pair_tiles, loc_bin):
    tiles, members, points = anomalies.shape
    slots = loc_bin.shape[0]
    size = lax.axis_size("tile")
    place = lax.axis_index("tile")
    to_u, to_v = routes(size, FROM_U), routes(size, FROM_V)
    send = lambda x, pairs: lax.ppermute(x, "tile", pairs)
    stay = lambda x: pltpu.with_memory_space_constraint(x, pltpu.HBM)
    swap = lambda x: lax.ppermute(x, "mem", [(0, 1), (1, 0)])

    sds = jax.ShapeDtypeStruct
    vm = pltpu.VMEM
    a_l = call(
        pack_kernel,
        sds((tiles * members + SLOT_ROWS, points), BF16),
        "hhh",
        [
            pltpu.SMEM((2, slots), jnp.int32),
            pltpu.SMEM((slots,), jnp.int32),
            pltpu.SemaphoreType.DMA((tiles + 2,)),
        ],
        1,
        stay(pair_tiles.T),
        stay(loc_bin),
        stay(anomalies),
    )
    a_v = send(a_l, to_v)
    a_u = send(a_l, to_u)
    a_t = swap(a_l)
    obs_tile, a_t = lax.optimization_barrier((obs_tile, a_t))
    forcing = call(
        forcing_kernel, sds(anomalies.shape, BF16), "sv", [vm(anomalies.shape, F32)], 1, obs_tile, stay(innovations)
    )
    g_v = send(forcing, to_v)
    g_u = send(forcing, to_u)
    other_list = jnp.where(place % 4 != 2, slot_codes(a_u, slots), slot_codes(a_v, slots))
    near, far_slots = entries_for(slot_codes(a_l, slots), other_list, place, tiles)
    square = vm((points, points), BF16)
    across = vm((points // WIDTH, points), F32)
    weights = [square, vm((NBIN, WIDTH, points), F32), across]
    weights_far = [vm((2, points, points), BF16), vm((2 * NBIN, WIDTH, points), F32), across]
    ints = pltpu.SMEM((slots,), jnp.int32)

    a_vt = swap(a_v)
    a_ut = swap(a_u)
    far, inc_u, inc_v = call(
        early_kernel,
        (sds((slots, points, points), BF16), sds(anomalies.shape, F32), sds(anomalies.shape, F32)),
        "vvvvvvvvv",
        [*weights_far, ints, ints],
        4,
        near,
        far_slots,
        a_l,
        a_t,
        a_u,
        a_ut,
        a_v,
        a_vt,
        forcing,
    )
    finish = lambda group, inc, g: call(
        functools.partial(far_kernel, group),
        sds(anomalies.shape, BF16),
        "vvvv",
        [vm(anomalies.shape, F32), ints, ints],
        1,
        far_slots,
        far,
        inc,
        g,
    )
    from_u = send(finish(1, inc_u, g_v), back(to_u))
    from_v = send(finish(2, inc_v, g_u), back(to_v))
    total = call(
        late_kernel,
        sds(anomalies.shape, F32),
        "vvvvvvvvvv",
        [*weights, ints],
        10,
        near,
        a_l,
        a_t,
        a_u,
        a_ut,
        a_v,
        a_vt,
        forcing,
        g_u,
        g_v,
    )
    return call(
        final_kernel,
        sds(anomalies.shape, BF16),
        "vvv",
        [vm(anomalies.shape, BF16), pltpu.SemaphoreType.DMA((tiles,))],
        1,
        total,
        from_v,
        from_u,
        to="h",
    )


def solution(mesh):
    return jax.shard_map(
        per_device,
        mesh=mesh,
        in_specs=(
            P("tile", "mem", None),
            P("tile", "mem", None),
            P("tile"),
            P("tile", None),
            P("tile"),
        ),
        out_specs=P("tile", "mem", None),
        check_vma=False,
    )
```

```python
import functools

import jax
import jax.numpy as jnp
from jax import lax
from jax.experimental import pallas as pl
from jax.experimental.pallas import tpu as pltpu
from jax.sharding import PartitionSpec as P

MEMBERS = 256
NBIN = 4
RADIUS = 4
WIDTH = 32
ROWS = 128
SLOT_ROWS = 16
F32 = jnp.float32
BF16 = jnp.bfloat16
VMEM_BYTES = 24 * 1024 * 1024
FULL_BYTES = 60 * 1024 * 1024

FROM_U = {0: 1, 1: 2, 2: 2}
FROM_V = {0: 2, 1: 4, 2: 1}


def routes(size, steps):
    return [(t + step, t) for t in range(size) for r, step in steps.items() if t % 4 == r and t + step < size]


def back(pairs):
    return [(b, a) for a, b in pairs]


def slot_codes(message, slots):
    rows = message.shape[0] - SLOT_ROWS
    parts = message[rows : rows + slots, :3].astype(jnp.int32)
    return parts[:, 0] + (parts[:, 1] << 8) + (parts[:, 2] << 16)


def entries_for(own, other, place, core, tiles):
    r = place % 4
    first, second = (own >> 8) & 255, own >> 16
    dist = second // tiles
    group = jnp.where(r == 0, dist, jnp.where(r == 2, 3 - dist, 1))
    group = jnp.where(core == 1, 3 - group, group)
    group = jnp.where(dist == 0, 0, group)
    entry = (own & 65535) + ((second % tiles + tiles * group) << 16)
    here = (dist == 0) | (r == 0) | (r == 2) | ((r == 1) & (dist == 2))
    near = jnp.where((own > 0) & here, entry, 0)
    first, second = (other >> 8) & 255, other >> 16
    dist = second // tiles
    second = second % tiles
    turned = (r == 2) != (core == 1)
    entry = (other & 255) + jnp.where(turned, 2 * NBIN, 0)
    entry = entry + (jnp.where(turned, second, first) << 8) + (jnp.where(turned, first, second) << 16)
    far = jnp.where((other > 0) & (r != 3) & (dist == jnp.where(r == 1, 2, 1)), entry, 0)
    return near[None], far[None]


def decode(entry):
    return lax.shift_right_logical(entry, 1) & 127, lax.shift_right_logical(entry, 8) & 255, lax.shift_right_logical(entry, 16)


def read_slots(entries, ints):
    row = entries[...]
    lane = lax.broadcasted_iota(jnp.int32, row.shape, 1)
    for k in range(row.shape[1]):
        ints[k] = jnp.max(jnp.where(lane == k, row, 0))


def fill_weights(along, across, points):
    q = lax.broadcasted_iota(jnp.int32, (WIDTH, points), 1) % WIDTH
    p = lax.broadcasted_iota(jnp.int32, (WIDTH, points), 0)
    gap = (q - p).astype(F32)
    for k in range(along.shape[0]):
        shift = (gap if k < NBIN else -gap) + 0.5 * RADIUS * (k % NBIN)
        along[k] = jnp.exp(-(shift * shift) / (2.0 * RADIUS * RADIUS))
    levels = points // WIDTH
    row = lax.broadcasted_iota(jnp.int32, (levels, points), 1) // WIDTH
    level = lax.broadcasted_iota(jnp.int32, (levels, points), 0)
    gap = (row - level).astype(F32)
    across[...] = jnp.exp(-(gap * gap) / (2.0 * RADIUS * RADIUS)) / (MEMBERS - 1)


def both(halves, tile, cols):
    rows = pl.ds(pl.multiple_of(tile * ROWS, ROWS), ROWS)
    return jnp.concatenate([half[rows, cols] for half in halves], axis=0)


def covariance(left, right, first, second, weight, across, out):
    points = out.shape[1]
    values = both(right, second, slice(None))
    for p0 in range(0, points, ROWS):
        cross = lax.dot_general(
            both(left, first, slice(p0, p0 + ROWS)), values, (((0,), (0,)), ((), ())), preferred_element_type=F32
        )
        for row in range(0, ROWS, WIDTH):
            level = (p0 + row) // WIDTH
            part = cross[row : row + WIDTH] * (weight * across[pl.ds(level, 1), :])
            out[pl.ds(p0 + row, WIDTH), :] = part.astype(BF16)


def to_first(g, c):
    return lax.dot_general(g, c, (((1,), (1,)), ((), ())), preferred_element_type=F32)


def to_second(g, c):
    return lax.dot_general(g, c, (((1,), (0,)), ((), ())), preferred_element_type=F32)


def pack_kernel(pairs, bins, anomalies, out, pairs_s, bins_s, sems):
    tiles, members = anomalies.shape[0], anomalies.shape[1]
    slots = bins.shape[0]
    copies = [pltpu.make_async_copy(pairs, pairs_s, sems.at[tiles]), pltpu.make_async_copy(bins, bins_s, sems.at[tiles + 1])]
    for t in range(tiles):
        copies.append(pltpu.make_async_copy(anomalies.at[t], out.at[pl.ds(t * members, members), :], sems.at[t]))
    for copy in copies:
        copy.start()
    copies[0].wait()
    copies[1].wait()
    row = lax.broadcasted_iota(jnp.int32, (SLOT_ROWS, 128), 0)
    lane = lax.broadcasted_iota(jnp.int32, (SLOT_ROWS, 128), 1)
    value = jnp.zeros(lane.shape, jnp.int32)
    for k in range(slots):
        first = lax.rem(pairs_s[0, k], tiles)
        second = pairs_s[1, k] - pairs_s[0, k] + first
        parts = jnp.where(lane == 0, 1 + 2 * bins_s[k], jnp.where(lane == 1, first, jnp.where(lane == 2, second, 0)))
        value = jnp.where((row == k) & (bins_s[k] < NBIN), parts, value)
    out[pl.ds(tiles * members, SLOT_ROWS), :] = jnp.zeros((SLOT_ROWS, out.shape[1]), BF16)
    out[pl.ds(tiles * members, SLOT_ROWS), pl.ds(0, 128)] = value.astype(F32).astype(BF16)
    for copy in copies[2:]:
        copy.wait()


def forcing_kernel(obs, innov, out, total):
    tiles = out.shape[0]
    total[...] = jnp.zeros_like(total)

    def step(o, carry):
        t = lax.rem(obs[o], tiles)
        total[t] = total[t] + innov[o].astype(F32)
        return carry

    lax.fori_loop(0, innov.shape[0], step, 0)
    out[...] = total[...].astype(BF16)


def compact(ints, wanted, kept):
    count = jnp.int32(0)
    for k in range(ints.shape[0]):
        kept[count] = ints[k]
        count = count + wanted(ints[k]).astype(jnp.int32)
    return count


def in_twos(count, step):
    def two(k, carry):
        step([2 * k, 2 * k + 1])
        return carry

    lax.fori_loop(0, lax.div(count, 2), two, 0)

    @pl.when(lax.rem(count, 2) == 1)
    def _():
        step([count - 1])


def add_near(group, ints, kept, left, right, g, inc, c, along, across):
    tiles = g.shape[0]

    def wanted(entry):
        _, _, second = decode(entry)
        return (entry > 0) & (second >= group * tiles) & (second < (group + 1) * tiles)

    def step(indices):
        pairs = [decode(kept[k]) for k in indices]
        for q, (bins, first, second) in enumerate(pairs):
            covariance(left, right, first, second - group * tiles, along[bins], across, c.at[q])
        parts = [to_second(g[first], c[q]) for q, (_, first, _) in enumerate(pairs)]
        for part, (_, _, second) in zip(parts, pairs):
            here = second - group * tiles
            inc[here] = inc[here] + part

    in_twos(compact(ints, wanted, kept), step)


def early_kernel(near, far_slots, lm, lt, um, ut, vm, vt, g, far, inc_u, inc_v, c, along, across, ints, kept):
    points = c.shape[1]
    read_slots(near, ints)
    fill_weights(along, across, points)
    inc_u[...] = jnp.zeros_like(inc_u)
    inc_v[...] = jnp.zeros_like(inc_v)
    add_near(1, ints, kept, (lm, lt), (um, ut), g, inc_u, c, along, across)
    add_near(2, ints, kept, (lm, lt), (vm, vt), g, inc_v, c, along, across)
    read_slots(far_slots, ints)

    def step(indices):
        for k in indices:
            bins, first, second = decode(kept[k])
            covariance((um, ut), (vm, vt), first, second, along[bins], across, far.at[k])

    in_twos(compact(ints, lambda entry: entry > 0, kept), step)


def far_kernel(group, far_slots, far, inc, g, out, total, ints, kept):
    read_slots(far_slots, ints)
    total[...] = inc[...]

    def step(indices):
        pairs = [decode(kept[k])[1:] for k in indices]
        if group == 1:
            parts = [to_first(g[second], far[k]) for k, (_, second) in zip(indices, pairs)]
            places = [first for first, _ in pairs]
        else:
            parts = [to_second(g[first], far[k]) for k, (first, _) in zip(indices, pairs)]
            places = [second for _, second in pairs]
        for part, here in zip(parts, places):
            total[here] = total[here] + part

    in_twos(compact(ints, lambda entry: entry > 0, kept), step)
    out[...] = total[...].astype(BF16)


def late_kernel(near, lm, lt, um, ut, vm, vt, g_l, g_u, g_v, out, c, along, across, near_s):
    read_slots(near, near_s)
    tiles, members, points = g_l.shape
    fill_weights(along, across, points)

    def own(t, carry):
        covariance((lm, lt), (lm, lt), t, t, along[0], across, c)
        rows = pl.ds(pl.multiple_of(t * members, members), members)
        out[t] = lm[rows, :].astype(F32) + to_first(g_l[t], c[...])
        return carry

    lax.fori_loop(0, tiles, own, 0)

    def pair(k, carry):
        entry = near_s[k]
        bins, first, second = decode(entry)

        for group, (right, g) in enumerate((((lm, lt), g_l), ((um, ut), g_u), ((vm, vt), g_v))):
            here = second - group * tiles

            @pl.when((entry > 0) & (here >= 0) & (here < tiles))
            def _():
                covariance((lm, lt), right, first, here, along[bins], across, c)
                out[first] = out[first] + to_first(g[here], c[...])
                if group == 0:
                    out[here] = out[here] + to_second(g_l[first], c[...])

        return carry

    lax.fori_loop(0, near.shape[1], pair, 0)


def final_kernel(total, from_u, from_v, out, done, sems):
    copies = []
    for t in range(total.shape[0]):
        done[t] = (total[t] + from_u[t].astype(F32) + from_v[t].astype(F32)).astype(BF16)
        copies.append(pltpu.make_async_copy(done.at[t], out.at[t], sems.at[t]))
        copies[-1].start()
    for copy in copies:
        copy.wait()


def call(kernel, outs, places, scratch, us, *args, grant=VMEM_BYTES, to="v"):
    spec = {"s": pl.BlockSpec(memory_space=pltpu.SMEM), "v": pl.BlockSpec(memory_space=pltpu.VMEM), "h": pl.BlockSpec(memory_space=pl.ANY), "d": pl.BlockSpec(memory_space=pltpu.HBM)}
    return pl.pallas_call(
        kernel,
        out_shape=outs,
        in_specs=[spec[p] for p in places],
        out_specs=jax.tree.map(lambda _: spec[to], outs),
        scratch_shapes=scratch,
        compiler_params=pltpu.CompilerParams(vmem_limit_bytes=grant),
        cost_estimate=pl.CostEstimate(flops=int(us * 1e7), bytes_accessed=int(us * 3e4), transcendentals=0),
    )(*args)


def per_device(anomalies, innovations, obs_tile, pair_tiles, loc_bin):
    tiles, members, points = anomalies.shape
    slots = loc_bin.shape[0]
    size = lax.axis_size("tile")
    place = lax.axis_index("tile")
    core = lax.axis_index("mem")
    routes_u, routes_v = routes(size, FROM_U), routes(size, FROM_V)
    to_u = routes_u + [(size + a, size + b) for a, b in routes_v]
    to_v = routes_v + [(size + a, size + b) for a, b in routes_u]
    send = lambda x, pairs: lax.ppermute(x, ("mem", "tile"), pairs)
    stay = lambda x: pltpu.with_memory_space_constraint(x, pltpu.HBM)
    swap = lambda x: lax.ppermute(x, "mem", [(0, 1), (1, 0)])

    sds = jax.ShapeDtypeStruct
    vm = pltpu.VMEM
    a_l = call(
        pack_kernel,
        sds((tiles * members + SLOT_ROWS, points), BF16),
        "hhh",
        [
            pltpu.SMEM((2, slots), jnp.int32),
            pltpu.SMEM((slots,), jnp.int32),
            pltpu.SemaphoreType.DMA((tiles + 2,)),
        ],
        1,
        stay(pair_tiles.T),
        stay(loc_bin),
        stay(anomalies),
    )
    a_v = send(a_l, to_v)
    a_u = send(a_l, to_u)
    a_t = swap(a_l)
    obs_tile, a_t = lax.optimization_barrier((obs_tile, a_t))
    forcing = call(
        forcing_kernel, sds(anomalies.shape, BF16), "sv", [vm(anomalies.shape, F32)], 1, obs_tile, stay(innovations)
    )
    g_v = send(forcing, to_v)
    g_u = send(forcing, to_u)
    other_list = jnp.where((place % 4 != 2) == (core == 0), slot_codes(a_u, slots), slot_codes(a_v, slots))
    near, far_slots = entries_for(slot_codes(a_l, slots), other_list, place, core, tiles)
    square = vm((points, points), BF16)
    across = vm((points // WIDTH, points), F32)
    weights = [square, vm((NBIN, WIDTH, points), F32), across]
    weights_far = [vm((2, points, points), BF16), vm((2 * NBIN, WIDTH, points), F32), across]
    ints = pltpu.SMEM((slots,), jnp.int32)

    a_vt = swap(a_u)
    a_ut = swap(a_v)
    far, inc_u, inc_v = call(
        early_kernel,
        (sds((slots, points, points), BF16), sds(anomalies.shape, F32), sds(anomalies.shape, F32)),
        "vvvvvvvvv",
        [*weights_far, ints, ints],
        4,
        near,
        far_slots,
        a_l,
        a_t,
        a_u,
        a_ut,
        a_v,
        a_vt,
        forcing,
    )
    finish = lambda group, inc, g: call(
        functools.partial(far_kernel, group),
        sds(anomalies.shape, BF16),
        "vvvv",
        [vm(anomalies.shape, F32), ints, ints],
        1,
        far_slots,
        far,
        inc,
        g,
    )
    from_u = send(finish(1, inc_u, g_v), back(to_u))
    from_v = send(finish(2, inc_v, g_u), back(to_v))
    total = call(
        late_kernel,
        sds(anomalies.shape, F32),
        "vvvvvvvvvv",
        [*weights, ints],
        10,
        near,
        a_l,
        a_t,
        a_u,
        a_ut,
        a_v,
        a_vt,
        forcing,
        g_u,
        g_v,
    )
    return call(
        final_kernel,
        sds(anomalies.shape, BF16),
        "vvv",
        [vm(anomalies.shape, BF16), pltpu.SemaphoreType.DMA((tiles,))],
        1,
        total,
        from_v,
        from_u,
        to="h",
    )


def solution(mesh):
    return jax.shard_map(
        per_device,
        mesh=mesh,
        in_specs=(
            P("tile", "mem", None),
            P("tile", "mem", None),
            P("tile"),
            P("tile", None),
            P("tile"),
        ),
        out_specs=P("tile", "mem", None),
        check_vma=False,
    )
```

```python
import functools

import jax
import jax.numpy as jnp
from jax import lax
from jax.experimental import pallas as pl
from jax.experimental.pallas import tpu as pltpu
from jax.sharding import PartitionSpec as P

MEMBERS = 256
NBIN = 4
RADIUS = 4
WIDTH = 32
ROWS = 128
SLOT_ROWS = 16
F32 = jnp.float32
BF16 = jnp.bfloat16
VMEM_BYTES = 24 * 1024 * 1024
FULL_BYTES = 60 * 1024 * 1024

FROM_U = {0: 1, 1: 2, 2: 2}
FROM_V = {0: 2, 1: 4, 2: 1}


def routes(size, steps):
    return [(t + step, t) for t in range(size) for r, step in steps.items() if t % 4 == r and t + step < size]


def back(pairs):
    return [(b, a) for a, b in pairs]


def slot_codes(message, slots):
    rows = message.shape[0] - SLOT_ROWS
    parts = message[rows : rows + slots, :3].astype(jnp.int32)
    return parts[:, 0] + (parts[:, 1] << 8) + (parts[:, 2] << 16)


def entries_for(own, other, place, core, tiles):
    r = place % 4
    first, second = (own >> 8) & 255, own >> 16
    dist = second // tiles
    group = jnp.where(r == 0, dist, jnp.where(r == 2, 3 - dist, 1))
    group = jnp.where(core == 1, 3 - group, group)
    group = jnp.where(dist == 0, 0, group)
    entry = (own & 65535) + ((second % tiles + tiles * group) << 16)
    here = (dist == 0) | (r == 0) | (r == 2) | ((r == 1) & (dist == 2))
    near = jnp.where((own > 0) & here, entry, 0)
    first, second = (other >> 8) & 255, other >> 16
    dist = second // tiles
    second = second % tiles
    turned = (r == 2) != (core == 1)
    entry = (other & 255) + jnp.where(turned, 2 * NBIN, 0)
    entry = entry + (jnp.where(turned, second, first) << 8) + (jnp.where(turned, first, second) << 16)
    far = jnp.where((other > 0) & (r != 3) & (dist == jnp.where(r == 1, 2, 1)), entry, 0)
    return near[None], far[None]


def decode(entry):
    return lax.shift_right_logical(entry, 1) & 127, lax.shift_right_logical(entry, 8) & 255, lax.shift_right_logical(entry, 16)


def read_slots(entries, ints):
    row = entries[...]
    lane = lax.broadcasted_iota(jnp.int32, row.shape, 1)
    for k in range(row.shape[1]):
        ints[k] = jnp.max(jnp.where(lane == k, row, 0))


def fill_weights(along, across, points):
    q = lax.broadcasted_iota(jnp.int32, (WIDTH, points), 1) % WIDTH
    p = lax.broadcasted_iota(jnp.int32, (WIDTH, points), 0)
    gap = (q - p).astype(F32)
    for k in range(along.shape[0]):
        shift = (gap if k < NBIN else -gap) + 0.5 * RADIUS * (k % NBIN)
        along[k] = jnp.exp(-(shift * shift) / (2.0 * RADIUS * RADIUS))
    levels = points // WIDTH
    row = lax.broadcasted_iota(jnp.int32, (levels, points), 1) // WIDTH
    level = lax.broadcasted_iota(jnp.int32, (levels, points), 0)
    gap = (row - level).astype(F32)
    across[...] = jnp.exp(-(gap * gap) / (2.0 * RADIUS * RADIUS)) / (MEMBERS - 1)


def both(halves, tile, cols):
    rows = pl.ds(pl.multiple_of(tile * ROWS, ROWS), ROWS)
    return jnp.concatenate([half[rows, cols] for half in halves], axis=0)


def covariance(left, right, first, second, weight, across, out):
    points = out.shape[1]
    values = both(right, second, slice(None))
    for p0 in range(0, points, ROWS):
        cross = lax.dot_general(
            both(left, first, slice(p0, p0 + ROWS)), values, (((0,), (0,)), ((), ())), preferred_element_type=F32
        )
        for row in range(0, ROWS, WIDTH):
            level = (p0 + row) // WIDTH
            part = cross[row : row + WIDTH] * (weight * across[pl.ds(level, 1), :])
            out[pl.ds(p0 + row, WIDTH), :] = part.astype(BF16)


def to_first(g, c):
    return lax.dot_general(g, c, (((1,), (1,)), ((), ())), preferred_element_type=F32)


def to_second(g, c):
    return lax.dot_general(g, c, (((1,), (0,)), ((), ())), preferred_element_type=F32)


def pack_kernel(pairs, bins, anomalies, out, pairs_s, bins_s, sems):
    tiles, members = anomalies.shape[0], anomalies.shape[1]
    slots = bins.shape[0]
    copies = [pltpu.make_async_copy(pairs, pairs_s, sems.at[tiles]), pltpu.make_async_copy(bins, bins_s, sems.at[tiles + 1])]
    for t in range(tiles):
        copies.append(pltpu.make_async_copy(anomalies.at[t], out.at[pl.ds(t * members, members), :], sems.at[t]))
    for copy in copies:
        copy.start()
    copies[0].wait()
    copies[1].wait()
    row = lax.broadcasted_iota(jnp.int32, (SLOT_ROWS, 128), 0)
    lane = lax.broadcasted_iota(jnp.int32, (SLOT_ROWS, 128), 1)
    value = jnp.zeros(lane.shape, jnp.int32)
    for k in range(slots):
        first = lax.rem(pairs_s[0, k], tiles)
        second = pairs_s[1, k] - pairs_s[0, k] + first
        parts = jnp.where(lane == 0, 1 + 2 * bins_s[k], jnp.where(lane == 1, first, jnp.where(lane == 2, second, 0)))
        value = jnp.where((row == k) & (bins_s[k] < NBIN), parts, value)
    out[pl.ds(tiles * members, SLOT_ROWS), :] = jnp.zeros((SLOT_ROWS, out.shape[1]), BF16)
    out[pl.ds(tiles * members, SLOT_ROWS), pl.ds(0, 128)] = value.astype(F32).astype(BF16)
    for copy in copies[2:]:
        copy.wait()


def forcing_kernel(obs, innov, out, total):
    tiles = out.shape[0]
    total[...] = jnp.zeros_like(total)

    def step(o, carry):
        t = lax.rem(obs[o], tiles)
        total[t] = total[t] + innov[o].astype(F32)
        return carry

    lax.fori_loop(0, innov.shape[0], step, 0)
    out[...] = total[...].astype(BF16)


def compact(ints, wanted, kept):
    count = jnp.int32(0)
    for k in range(ints.shape[0]):
        kept[count] = ints[k]
        count = count + wanted(ints[k]).astype(jnp.int32)
    return count


def in_twos(count, step):
    def two(k, carry):
        step([2 * k, 2 * k + 1])
        return carry

    lax.fori_loop(0, lax.div(count, 2), two, 0)

    @pl.when(lax.rem(count, 2) == 1)
    def _():
        step([count - 1])


def add_near(group, ints, kept, left, right, g, inc, c, along, across):
    tiles = g.shape[0]

    def wanted(entry):
        _, _, second = decode(entry)
        return (entry > 0) & (second >= group * tiles) & (second < (group + 1) * tiles)

    def step(indices):
        pairs = [decode(kept[k]) for k in indices]
        for q, (bins, first, second) in enumerate(pairs):
            covariance(left, right, first, second - group * tiles, along[bins], across, c.at[q])
        parts = [to_second(g[first], c[q]) for q, (_, first, _) in enumerate(pairs)]
        for part, (_, _, second) in zip(parts, pairs):
            here = second - group * tiles
            inc[here] = inc[here] + part

    in_twos(compact(ints, wanted, kept), step)


def early_kernel(near, far_slots, lm, lt, um, ut, vm, vt, g, far, inc_u, inc_v, c, along, across, ints, kept):
    points = c.shape[1]
    read_slots(near, ints)
    fill_weights(along, across, points)
    inc_u[...] = jnp.zeros_like(inc_u)
    inc_v[...] = jnp.zeros_like(inc_v)
    add_near(1, ints, kept, (lm, lt), (um, ut), g, inc_u, c, along, across)
    add_near(2, ints, kept, (lm, lt), (vm, vt), g, inc_v, c, along, across)
    read_slots(far_slots, ints)

    def step(indices):
        for k in indices:
            bins, first, second = decode(kept[k])
            covariance((um, ut), (vm, vt), first, second, along[bins], across, far.at[k])

    in_twos(compact(ints, lambda entry: entry > 0, kept), step)


def far_kernel(group, far_slots, far, inc, g, out, total, ints, kept):
    read_slots(far_slots, ints)
    total[...] = inc[...]

    def step(indices):
        pairs = [decode(kept[k])[1:] for k in indices]
        if group == 1:
            parts = [to_first(g[second], far[k]) for k, (_, second) in zip(indices, pairs)]
            places = [first for first, _ in pairs]
        else:
            parts = [to_second(g[first], far[k]) for k, (first, _) in zip(indices, pairs)]
            places = [second for _, second in pairs]
        for part, here in zip(parts, places):
            total[here] = total[here] + part

    in_twos(compact(ints, lambda entry: entry > 0, kept), step)
    out[...] = total[...].astype(BF16)


def late_kernel(near, lm, lt, um, ut, vm, vt, g_l, g_u, g_v, out, c, along, across, near_s):
    read_slots(near, near_s)
    tiles, members, points = g_l.shape
    fill_weights(along, across, points)

    def own(t, carry):
        covariance((lm, lt), (lm, lt), t, t, along[0], across, c)
        rows = pl.ds(pl.multiple_of(t * members, members), members)
        out[t] = lm[rows, :].astype(F32) + to_first(g_l[t], c[...])
        return carry

    lax.fori_loop(0, tiles, own, 0)

    def pair(k, carry):
        entry = near_s[k]
        bins, first, second = decode(entry)

        for group, (right, g) in enumerate((((lm, lt), g_l), ((um, ut), g_u), ((vm, vt), g_v))):
            here = second - group * tiles

            @pl.when((entry > 0) & (here >= 0) & (here < tiles))
            def _():
                covariance((lm, lt), right, first, here, along[bins], across, c)
                out[first] = out[first] + to_first(g[here], c[...])
                if group == 0:
                    out[here] = out[here] + to_second(g_l[first], c[...])

        return carry

    lax.fori_loop(0, near.shape[1], pair, 0)


def final_kernel(total, from_u, from_v, out, done, sems):
    copies = []
    for t in range(total.shape[0]):
        done[t] = (total[t] + from_u[t].astype(F32) + from_v[t].astype(F32)).astype(BF16)
        copies.append(pltpu.make_async_copy(done.at[t], out.at[t], sems.at[t]))
        copies[-1].start()
    for copy in copies:
        copy.wait()


def call(kernel, outs, places, scratch, us, *args, grant=VMEM_BYTES, to="v"):
    spec = {"s": pl.BlockSpec(memory_space=pltpu.SMEM), "v": pl.BlockSpec(memory_space=pltpu.VMEM), "h": pl.BlockSpec(memory_space=pl.ANY), "d": pl.BlockSpec(memory_space=pltpu.HBM)}
    return pl.pallas_call(
        kernel,
        out_shape=outs,
        in_specs=[spec[p] for p in places],
        out_specs=jax.tree.map(lambda _: spec[to], outs),
        scratch_shapes=scratch,
        compiler_params=pltpu.CompilerParams(vmem_limit_bytes=grant),
        cost_estimate=pl.CostEstimate(flops=int(us * 1e7), bytes_accessed=int(us * 3e4), transcendentals=0),
    )(*args)


def per_device(anomalies, innovations, obs_tile, pair_tiles, loc_bin):
    tiles, members, points = anomalies.shape
    slots = loc_bin.shape[0]
    size = lax.axis_size("tile")
    place = lax.axis_index("tile")
    core = lax.axis_index("mem")
    routes_u, routes_v = routes(size, FROM_U), routes(size, FROM_V)
    to_u = routes_u + [(size + a, size + b) for a, b in routes_v]
    to_v = routes_v + [(size + a, size + b) for a, b in routes_u]
    send = lambda x, pairs: lax.ppermute(x, ("mem", "tile"), pairs)
    stay = lambda x: pltpu.with_memory_space_constraint(x, pltpu.HBM)
    swap = lambda x: lax.ppermute(x, "mem", [(0, 1), (1, 0)])

    sds = jax.ShapeDtypeStruct
    vm = pltpu.VMEM
    a_l = call(
        pack_kernel,
        sds((tiles * members + SLOT_ROWS, points), BF16),
        "hhh",
        [
            pltpu.SMEM((2, slots), jnp.int32),
            pltpu.SMEM((slots,), jnp.int32),
            pltpu.SemaphoreType.DMA((tiles + 2,)),
        ],
        1,
        stay(pair_tiles.T),
        stay(loc_bin),
        stay(anomalies),
    )
    a_v = send(a_l, to_v)
    a_u = send(a_l, to_u)
    a_t = swap(a_l)
    obs_tile, a_t = lax.optimization_barrier((obs_tile, a_t))
    forcing = call(
        forcing_kernel, sds(anomalies.shape, BF16), "sv", [vm(anomalies.shape, F32)], 1, obs_tile, stay(innovations)
    )
    g_v = send(forcing, to_v)
    late_forcing, a_v = lax.optimization_barrier((forcing, a_v))
    g_u = send(late_forcing, to_u)
    other_list = jnp.where((place % 4 != 2) == (core == 0), slot_codes(a_u, slots), slot_codes(a_v, slots))
    near, far_slots = entries_for(slot_codes(a_l, slots), other_list, place, core, tiles)
    square = vm((points, points), BF16)
    across = vm((points // WIDTH, points), F32)
    weights = [square, vm((NBIN, WIDTH, points), F32), across]
    weights_far = [vm((2, points, points), BF16), vm((2 * NBIN, WIDTH, points), F32), across]
    ints = pltpu.SMEM((slots,), jnp.int32)

    a_vt = swap(a_u)
    a_ut = swap(a_v)
    far, inc_u, inc_v = call(
        early_kernel,
        (sds((slots, points, points), BF16), sds(anomalies.shape, F32), sds(anomalies.shape, F32)),
        "vvvvvvvvv",
        [*weights_far, ints, ints],
        4,
        near,
        far_slots,
        a_l,
        a_t,
        a_u,
        a_ut,
        a_v,
        a_vt,
        forcing,
    )
    finish = lambda group, inc, g: call(
        functools.partial(far_kernel, group),
        sds(anomalies.shape, BF16),
        "vvvv",
        [vm(anomalies.shape, F32), ints, ints],
        1,
        far_slots,
        far,
        inc,
        g,
    )
    from_u = send(finish(1, inc_u, g_v), back(to_u))
    from_v = send(finish(2, inc_v, g_u), back(to_v))
    total = call(
        late_kernel,
        sds(anomalies.shape, F32),
        "vvvvvvvvvv",
        [*weights, ints],
        10,
        near,
        a_l,
        a_t,
        a_u,
        a_ut,
        a_v,
        a_vt,
        forcing,
        g_u,
        g_v,
    )
    return call(
        final_kernel,
        sds(anomalies.shape, BF16),
        "vvv",
        [vm(anomalies.shape, BF16), pltpu.SemaphoreType.DMA((tiles,))],
        1,
        total,
        from_v,
        from_u,
        to="h",
    )


def solution(mesh):
    return jax.shard_map(
        per_device,
        mesh=mesh,
        in_specs=(
            P("tile", "mem", None),
            P("tile", "mem", None),
            P("tile"),
            P("tile", None),
            P("tile"),
        ),
        out_specs=P("tile", "mem", None),
        check_vma=False,
    )
```

```python
import functools

import jax
import jax.numpy as jnp
from jax import lax
from jax.experimental import pallas as pl
from jax.experimental.pallas import tpu as pltpu
from jax.sharding import PartitionSpec as P

MEMBERS = 256
NBIN = 4
RADIUS = 4
WIDTH = 32
ROWS = 128
SLOT_ROWS = 16
F32 = jnp.float32
BF16 = jnp.bfloat16
VMEM_BYTES = 24 * 1024 * 1024
FULL_BYTES = 60 * 1024 * 1024

FROM_U = {0: 1, 1: 2, 2: 2}
FROM_V = {0: 2, 1: 4, 2: 1}


def routes(size, steps):
    return [(t + step, t) for t in range(size) for r, step in steps.items() if t % 4 == r and t + step < size]


def back(pairs):
    return [(b, a) for a, b in pairs]


def slot_codes(message, slots):
    rows = message.shape[0] - SLOT_ROWS
    parts = message[rows : rows + slots, :3].astype(jnp.int32)
    return parts[:, 0] + (parts[:, 1] << 8) + (parts[:, 2] << 16)


def entries_for(own, other, place, core, tiles):
    r = place % 4
    first, second = (own >> 8) & 255, own >> 16
    dist = second // tiles
    group = jnp.where(r == 0, dist, jnp.where(r == 2, 3 - dist, 1))
    group = jnp.where(core == 1, 3 - group, group)
    group = jnp.where(dist == 0, 0, group)
    entry = (own & 65535) + ((second % tiles + tiles * group) << 16)
    here = (dist == 0) | (r == 0) | (r == 2) | ((r == 1) & (dist == 2))
    near = jnp.where((own > 0) & here, entry, 0)
    first, second = (other >> 8) & 255, other >> 16
    dist = second // tiles
    second = second % tiles
    turned = (r == 2) != (core == 1)
    entry = (other & 255) + jnp.where(turned, 2 * NBIN, 0)
    entry = entry + (jnp.where(turned, second, first) << 8) + (jnp.where(turned, first, second) << 16)
    far = jnp.where((other > 0) & (r != 3) & (dist == jnp.where(r == 1, 2, 1)), entry, 0)
    return near[None], far[None]


def decode(entry):
    return lax.shift_right_logical(entry, 1) & 127, lax.shift_right_logical(entry, 8) & 255, lax.shift_right_logical(entry, 16)


def read_slots(entries, ints):
    row = entries[...]
    lane = lax.broadcasted_iota(jnp.int32, row.shape, 1)
    for k in range(row.shape[1]):
        ints[k] = jnp.max(jnp.where(lane == k, row, 0))


def fill_weights(along, across, points):
    q = lax.broadcasted_iota(jnp.int32, (WIDTH, points), 1) % WIDTH
    p = lax.broadcasted_iota(jnp.int32, (WIDTH, points), 0)
    gap = (q - p).astype(F32)
    for k in range(along.shape[0]):
        shift = (gap if k < NBIN else -gap) + 0.5 * RADIUS * (k % NBIN)
        along[k] = jnp.exp(-(shift * shift) / (2.0 * RADIUS * RADIUS))
    levels = points // WIDTH
    row = lax.broadcasted_iota(jnp.int32, (levels, points), 1) // WIDTH
    level = lax.broadcasted_iota(jnp.int32, (levels, points), 0)
    gap = (row - level).astype(F32)
    across[...] = jnp.exp(-(gap * gap) / (2.0 * RADIUS * RADIUS)) / (MEMBERS - 1)


def both(halves, tile, cols):
    rows = pl.ds(pl.multiple_of(tile * ROWS, ROWS), ROWS)
    return jnp.concatenate([half[rows, cols] for half in halves], axis=0)


def covariance(left, right, first, second, weight, across, out):
    points = out.shape[1]
    values = both(right, second, slice(None))
    for p0 in range(0, points, ROWS):
        cross = lax.dot_general(
            both(left, first, slice(p0, p0 + ROWS)), values, (((0,), (0,)), ((), ())), preferred_element_type=F32
        )
        for row in range(0, ROWS, WIDTH):
            level = (p0 + row) // WIDTH
            part = cross[row : row + WIDTH] * (weight * across[pl.ds(level, 1), :])
            out[pl.ds(p0 + row, WIDTH), :] = part.astype(BF16)


def to_first(g, c):
    return lax.dot_general(g, c, (((1,), (1,)), ((), ())), preferred_element_type=F32)


def to_second(g, c):
    return lax.dot_general(g, c, (((1,), (0,)), ((), ())), preferred_element_type=F32)


def pack_kernel(pairs, bins, anomalies, out, pairs_s, bins_s, sems):
    tiles, members = anomalies.shape[0], anomalies.shape[1]
    slots = bins.shape[0]
    copies = [pltpu.make_async_copy(pairs, pairs_s, sems.at[tiles]), pltpu.make_async_copy(bins, bins_s, sems.at[tiles + 1])]
    for t in range(tiles):
        copies.append(pltpu.make_async_copy(anomalies.at[t], out.at[pl.ds(t * members, members), :], sems.at[t]))
    for copy in copies:
        copy.start()
    copies[0].wait()
    copies[1].wait()
    row = lax.broadcasted_iota(jnp.int32, (SLOT_ROWS, 128), 0)
    lane = lax.broadcasted_iota(jnp.int32, (SLOT_ROWS, 128), 1)
    value = jnp.zeros(lane.shape, jnp.int32)
    for k in range(slots):
        first = lax.rem(pairs_s[0, k], tiles)
        second = pairs_s[1, k] - pairs_s[0, k] + first
        parts = jnp.where(lane == 0, 1 + 2 * bins_s[k], jnp.where(lane == 1, first, jnp.where(lane == 2, second, 0)))
        value = jnp.where((row == k) & (bins_s[k] < NBIN), parts, value)
    out[pl.ds(tiles * members, SLOT_ROWS), :] = jnp.zeros((SLOT_ROWS, out.shape[1]), BF16)
    out[pl.ds(tiles * members, SLOT_ROWS), pl.ds(0, 128)] = value.astype(F32).astype(BF16)
    for copy in copies[2:]:
        copy.wait()


def forcing_kernel(obs, innov, out, total):
    tiles = out.shape[0]
    total[...] = jnp.zeros_like(total)

    def step(o, carry):
        t = lax.rem(obs[o], tiles)
        total[t] = total[t] + innov[o].astype(F32)
        return carry

    lax.fori_loop(0, innov.shape[0], step, 0)
    out[...] = total[...].astype(BF16)


def compact(ints, wanted, kept):
    count = jnp.int32(0)
    for k in range(ints.shape[0]):
        kept[count] = ints[k]
        count = count + wanted(ints[k]).astype(jnp.int32)
    return count


def in_twos(count, step):
    def two(k, carry):
        step([2 * k, 2 * k + 1])
        return carry

    lax.fori_loop(0, lax.div(count, 2), two, 0)

    @pl.when(lax.rem(count, 2) == 1)
    def _():
        step([count - 1])


def add_near(group, ints, kept, left, right, g, inc, c, along, across):
    tiles = g.shape[0]

    def wanted(entry):
        _, _, second = decode(entry)
        return (entry > 0) & (second >= group * tiles) & (second < (group + 1) * tiles)

    def step(indices):
        pairs = [decode(kept[k]) for k in indices]
        for q, (bins, first, second) in enumerate(pairs):
            covariance(left, right, first, second - group * tiles, along[bins], across, c.at[q])
        parts = [to_second(g[first], c[q]) for q, (_, first, _) in enumerate(pairs)]
        for part, (_, _, second) in zip(parts, pairs):
            here = second - group * tiles
            inc[here] = inc[here] + part

    in_twos(compact(ints, wanted, kept), step)


def early_kernel(near, far_slots, lm, lt, um, ut, vm, vt, g, far, inc_u, inc_v, c, along, across, ints, kept):
    points = c.shape[1]
    read_slots(near, ints)
    fill_weights(along, across, points)
    inc_u[...] = jnp.zeros_like(inc_u)
    inc_v[...] = jnp.zeros_like(inc_v)
    add_near(1, ints, kept, (lm, lt), (um, ut), g, inc_u, c, along, across)
    add_near(2, ints, kept, (lm, lt), (vm, vt), g, inc_v, c, along, across)
    read_slots(far_slots, ints)

    def step(indices):
        for k in indices:
            bins, first, second = decode(kept[k])
            covariance((um, ut), (vm, vt), first, second, along[bins], across, far.at[k])

    in_twos(compact(ints, lambda entry: entry > 0, kept), step)


def far_kernel(group, far_slots, far, inc, g, out, total, ints, kept):
    read_slots(far_slots, ints)
    total[...] = inc[...]

    def step(indices):
        pairs = [decode(kept[k])[1:] for k in indices]
        if group == 1:
            parts = [to_first(g[second], far[k]) for k, (_, second) in zip(indices, pairs)]
            places = [first for first, _ in pairs]
        else:
            parts = [to_second(g[first], far[k]) for k, (first, _) in zip(indices, pairs)]
            places = [second for _, second in pairs]
        for part, here in zip(parts, places):
            total[here] = total[here] + part

    in_twos(compact(ints, lambda entry: entry > 0, kept), step)
    out[...] = total[...].astype(BF16)


def late_kernel(near, lm, lt, um, ut, vm, vt, g_l, g_u, g_v, out, c, along, across, ints, kept):
    tiles, members, points = g_l.shape
    read_slots(near, ints)
    fill_weights(along, across, points)

    def own(k, carry):
        for q in range(2):
            covariance((lm, lt), (lm, lt), 2 * k + q, 2 * k + q, along[0], across, c.at[q])
        for q in range(2):
            t = 2 * k + q
            rows = pl.ds(pl.multiple_of(t * members, members), members)
            out[t] = lm[rows, :].astype(F32) + to_first(g_l[t], c[q])
        return carry

    lax.fori_loop(0, tiles // 2, own, 0)

    for group, right, g in ((0, (lm, lt), g_l), (1, (um, ut), g_u), (2, (vm, vt), g_v)):

        def wanted(entry):
            _, _, second = decode(entry)
            return (entry > 0) & (second >= group * tiles) & (second < (group + 1) * tiles)

        def step(indices):
            pairs = [decode(kept[k]) for k in indices]
            for q, (bins, first, second) in enumerate(pairs):
                covariance((lm, lt), right, first, second - group * tiles, along[bins], across, c.at[q])
            parts = [to_first(g[second - group * tiles], c[q]) for q, (_, _, second) in enumerate(pairs)]
            places = [first for _, first, _ in pairs]
            if group == 0:
                parts += [to_second(g_l[first], c[q]) for q, (_, first, _) in enumerate(pairs)]
                places += [second for _, _, second in pairs]
            for part, here in zip(parts, places):
                out[here] = out[here] + part

        in_twos(compact(ints, wanted, kept), step)


def final_kernel(total, from_u, from_v, out, done, sems):
    copies = []
    for t in range(total.shape[0]):
        done[t] = (total[t] + from_u[t].astype(F32) + from_v[t].astype(F32)).astype(BF16)
        copies.append(pltpu.make_async_copy(done.at[t], out.at[t], sems.at[t]))
        copies[-1].start()
    for copy in copies:
        copy.wait()


def call(kernel, outs, places, scratch, us, *args, grant=VMEM_BYTES, to="v"):
    spec = {"s": pl.BlockSpec(memory_space=pltpu.SMEM), "v": pl.BlockSpec(memory_space=pltpu.VMEM), "h": pl.BlockSpec(memory_space=pl.ANY), "d": pl.BlockSpec(memory_space=pltpu.HBM)}
    return pl.pallas_call(
        kernel,
        out_shape=outs,
        in_specs=[spec[p] for p in places],
        out_specs=jax.tree.map(lambda _: spec[to], outs),
        scratch_shapes=scratch,
        compiler_params=pltpu.CompilerParams(vmem_limit_bytes=grant),
        cost_estimate=pl.CostEstimate(flops=int(us * 1e7), bytes_accessed=int(us * 3e4), transcendentals=0),
    )(*args)


def per_device(anomalies, innovations, obs_tile, pair_tiles, loc_bin):
    tiles, members, points = anomalies.shape
    slots = loc_bin.shape[0]
    size = lax.axis_size("tile")
    place = lax.axis_index("tile")
    core = lax.axis_index("mem")
    routes_u, routes_v = routes(size, FROM_U), routes(size, FROM_V)
    to_u = routes_u + [(size + a, size + b) for a, b in routes_v]
    to_v = routes_v + [(size + a, size + b) for a, b in routes_u]
    send = lambda x, pairs: lax.ppermute(x, ("mem", "tile"), pairs)
    stay = lambda x: pltpu.with_memory_space_constraint(x, pltpu.HBM)
    swap = lambda x: lax.ppermute(x, "mem", [(0, 1), (1, 0)])

    sds = jax.ShapeDtypeStruct
    vm = pltpu.VMEM
    a_l = call(
        pack_kernel,
        sds((tiles * members + SLOT_ROWS, points), BF16),
        "hhh",
        [
            pltpu.SMEM((2, slots), jnp.int32),
            pltpu.SMEM((slots,), jnp.int32),
            pltpu.SemaphoreType.DMA((tiles + 2,)),
        ],
        1,
        stay(pair_tiles.T),
        stay(loc_bin),
        stay(anomalies),
    )
    a_v = send(a_l, to_v)
    a_u = send(a_l, to_u)
    a_t = swap(a_l)
    obs_tile, a_t = lax.optimization_barrier((obs_tile, a_t))
    forcing = call(
        forcing_kernel, sds(anomalies.shape, BF16), "sv", [vm(anomalies.shape, F32)], 1, obs_tile, stay(innovations)
    )
    g_v = send(forcing, to_v)
    late_forcing, a_v = lax.optimization_barrier((forcing, a_v))
    g_u = send(late_forcing, to_u)
    other_list = jnp.where((place % 4 != 2) == (core == 0), slot_codes(a_u, slots), slot_codes(a_v, slots))
    near, far_slots = entries_for(slot_codes(a_l, slots), other_list, place, core, tiles)
    square = vm((points, points), BF16)
    across = vm((points // WIDTH, points), F32)
    weights = [square, vm((NBIN, WIDTH, points), F32), across]
    weights_far = [vm((2, points, points), BF16), vm((2 * NBIN, WIDTH, points), F32), across]
    ints = pltpu.SMEM((slots,), jnp.int32)

    a_vt = swap(a_u)
    a_ut = swap(a_v)
    far, inc_u, inc_v = call(
        early_kernel,
        (sds((slots, points, points), BF16), sds(anomalies.shape, F32), sds(anomalies.shape, F32)),
        "vvvvvvvvv",
        [*weights_far, ints, ints],
        4,
        near,
        far_slots,
        a_l,
        a_t,
        a_u,
        a_ut,
        a_v,
        a_vt,
        forcing,
    )
    finish = lambda group, inc, g: call(
        functools.partial(far_kernel, group),
        sds(anomalies.shape, BF16),
        "vvvv",
        [vm(anomalies.shape, F32), ints, ints],
        1,
        far_slots,
        far,
        inc,
        g,
    )
    from_u = send(finish(1, inc_u, g_v), back(to_u))
    from_v = send(finish(2, inc_v, g_u), back(to_v))
    total = call(
        late_kernel,
        sds(anomalies.shape, F32),
        "vvvvvvvvvv",
        [vm((2, points, points), BF16), *weights[1:], ints, ints],
        10,
        near,
        a_l,
        a_t,
        a_u,
        a_ut,
        a_v,
        a_vt,
        forcing,
        g_u,
        g_v,
    )
    return call(
        final_kernel,
        sds(anomalies.shape, BF16),
        "vvv",
        [vm(anomalies.shape, BF16), pltpu.SemaphoreType.DMA((tiles,))],
        1,
        total,
        from_v,
        from_u,
        to="h",
    )


def solution(mesh):
    return jax.shard_map(
        per_device,
        mesh=mesh,
        in_specs=(
            P("tile", "mem", None),
            P("tile", "mem", None),
            P("tile"),
            P("tile", None),
            P("tile"),
        ),
        out_specs=P("tile", "mem", None),
        check_vma=False,
    )
```

```python
import functools

import jax
import jax.numpy as jnp
from jax import lax
from jax.experimental import pallas as pl
from jax.experimental.pallas import tpu as pltpu
from jax.sharding import PartitionSpec as P

MEMBERS = 256
NBIN = 4
RADIUS = 4
WIDTH = 32
ROWS = 128
SLOT_ROWS = 16
F32 = jnp.float32
BF16 = jnp.bfloat16
VMEM_BYTES = 24 * 1024 * 1024
FULL_BYTES = 60 * 1024 * 1024

FROM_U = {0: 1, 1: 2, 2: 2}
FROM_V = {0: 2, 1: 4, 2: 1}


def routes(size, steps):
    return [(t + step, t) for t in range(size) for r, step in steps.items() if t % 4 == r and t + step < size]


def back(pairs):
    return [(b, a) for a, b in pairs]


def slot_codes(message, slots):
    rows = message.shape[0] - SLOT_ROWS
    parts = message[rows : rows + slots, :3].astype(jnp.int32)
    return parts[:, 0] + (parts[:, 1] << 8) + (parts[:, 2] << 16)


def entries_for(own, other, place, core, tiles):
    r = place % 4
    first, second = (own >> 8) & 255, own >> 16
    dist = second // tiles
    group = jnp.where(r == 0, dist, jnp.where(r == 2, 3 - dist, 1))
    group = jnp.where(core == 1, 3 - group, group)
    group = jnp.where(dist == 0, 0, group)
    entry = (own & 65535) + ((second % tiles + tiles * group) << 16)
    here = (dist == 0) | (r == 0) | (r == 2) | ((r == 1) & (dist == 2))
    near = jnp.where((own > 0) & here, entry, 0)
    first, second = (other >> 8) & 255, other >> 16
    dist = second // tiles
    second = second % tiles
    turned = (r == 2) != (core == 1)
    entry = (other & 255) + jnp.where(turned, 2 * NBIN, 0)
    entry = entry + (jnp.where(turned, second, first) << 8) + (jnp.where(turned, first, second) << 16)
    far = jnp.where((other > 0) & (r != 3) & (dist == jnp.where(r == 1, 2, 1)), entry, 0)
    return near[None], far[None]


def decode(entry):
    return lax.shift_right_logical(entry, 1) & 127, lax.shift_right_logical(entry, 8) & 255, lax.shift_right_logical(entry, 16)


def read_slots(entries, ints):
    row = entries[...]
    lane = lax.broadcasted_iota(jnp.int32, row.shape, 1)
    for k in range(row.shape[1]):
        ints[k] = jnp.max(jnp.where(lane == k, row, 0))


def fill_weights(along, across, points):
    q = lax.broadcasted_iota(jnp.int32, (WIDTH, points), 1) % WIDTH
    p = lax.broadcasted_iota(jnp.int32, (WIDTH, points), 0)
    gap = (q - p).astype(F32)
    for k in range(along.shape[0]):
        shift = (gap if k < NBIN else -gap) + 0.5 * RADIUS * (k % NBIN)
        along[k] = jnp.exp(-(shift * shift) / (2.0 * RADIUS * RADIUS))
    levels = points // WIDTH
    row = lax.broadcasted_iota(jnp.int32, (levels, points), 1) // WIDTH
    level = lax.broadcasted_iota(jnp.int32, (levels, points), 0)
    gap = (row - level).astype(F32)
    across[...] = jnp.exp(-(gap * gap) / (2.0 * RADIUS * RADIUS)) / (MEMBERS - 1)


def both(halves, tile, blocks, count):
    span = (halves[0].shape[0] - SLOT_ROWS) // count
    parts = []
    for half in halves:
        rows = [pl.ds(pl.multiple_of(block * span + tile * ROWS, ROWS), ROWS) for block in blocks]
        parts.append(jnp.concatenate([half[r, :] for r in rows], axis=1))
    return jnp.concatenate(parts, axis=0)


def covariance(left, right, first, second, weight, across, out):
    points = out.shape[1]
    count = points // ROWS
    values = both(right, second, range(count), count)
    for p0 in range(0, points, ROWS):
        cross = lax.dot_general(
            both(left, first, [p0 // ROWS], count), values, (((0,), (0,)), ((), ())), preferred_element_type=F32
        )
        for row in range(0, ROWS, WIDTH):
            level = (p0 + row) // WIDTH
            part = cross[row : row + WIDTH] * (weight * across[pl.ds(level, 1), :])
            out[pl.ds(p0 + row, WIDTH), :] = part.astype(BF16)


def to_first(g, c):
    return lax.dot_general(g, c, (((1,), (1,)), ((), ())), preferred_element_type=F32)


def to_second(g, c):
    return lax.dot_general(g, c, (((1,), (0,)), ((), ())), preferred_element_type=F32)


def pack_kernel(pairs, bins, anomalies, out, pairs_s, bins_s, sems):
    tiles, members = anomalies.shape[0], anomalies.shape[1]
    slots = bins.shape[0]
    copies = [pltpu.make_async_copy(pairs, pairs_s, sems.at[0]), pltpu.make_async_copy(bins, bins_s, sems.at[1])]
    count = anomalies.shape[2] // ROWS
    for t in range(tiles):
        for block in range(count):
            rows = pl.ds((block * tiles + t) * members, members)
            source = anomalies.at[t, :, pl.ds(block * ROWS, ROWS)]
            copies.append(pltpu.make_async_copy(source, out.at[rows, :], sems.at[2 + t * count + block]))
    for copy in copies:
        copy.start()
    copies[0].wait()
    copies[1].wait()
    row = lax.broadcasted_iota(jnp.int32, (SLOT_ROWS, 128), 0)
    lane = lax.broadcasted_iota(jnp.int32, (SLOT_ROWS, 128), 1)
    value = jnp.zeros(lane.shape, jnp.int32)
    for k in range(slots):
        first = lax.rem(pairs_s[0, k], tiles)
        second = pairs_s[1, k] - pairs_s[0, k] + first
        parts = jnp.where(lane == 0, 1 + 2 * bins_s[k], jnp.where(lane == 1, first, jnp.where(lane == 2, second, 0)))
        value = jnp.where((row == k) & (bins_s[k] < NBIN), parts, value)
    out[pl.ds(count * tiles * members, SLOT_ROWS), :] = value.astype(F32).astype(BF16)
    for copy in copies[2:]:
        copy.wait()


def forcing_kernel(obs, innov, out, total):
    tiles = out.shape[0]
    total[...] = jnp.zeros_like(total)

    def step(o, carry):
        t = lax.rem(obs[o], tiles)
        total[t] = total[t] + innov[o].astype(F32)
        return carry

    lax.fori_loop(0, innov.shape[0], step, 0)
    out[...] = total[...].astype(BF16)


def compact(ints, wanted, kept):
    count = jnp.int32(0)
    for k in range(ints.shape[0]):
        kept[count] = ints[k]
        count = count + wanted(ints[k]).astype(jnp.int32)
    return count


def in_twos(count, step):
    def two(k, carry):
        step([2 * k, 2 * k + 1])
        return carry

    lax.fori_loop(0, lax.div(count, 2), two, 0)

    @pl.when(lax.rem(count, 2) == 1)
    def _():
        step([count - 1])


def add_near(group, ints, kept, left, right, g, inc, c, along, across):
    tiles = g.shape[0]

    def wanted(entry):
        _, _, second = decode(entry)
        return (entry > 0) & (second >= group * tiles) & (second < (group + 1) * tiles)

    def step(indices):
        pairs = [decode(kept[k]) for k in indices]
        for q, (bins, first, second) in enumerate(pairs):
            covariance(left, right, first, second - group * tiles, along[bins], across, c.at[q])
        parts = [to_second(g[first], c[q]) for q, (_, first, _) in enumerate(pairs)]
        for part, (_, _, second) in zip(parts, pairs):
            here = second - group * tiles
            inc[here] = inc[here] + part

    in_twos(compact(ints, wanted, kept), step)


def early_kernel(near, far_slots, lm, lt, um, ut, vm, vt, g, far, inc_u, inc_v, c, along, across, ints, kept):
    points = c.shape[1]
    read_slots(near, ints)
    fill_weights(along, across, points)
    inc_u[...] = jnp.zeros_like(inc_u)
    inc_v[...] = jnp.zeros_like(inc_v)
    add_near(1, ints, kept, (lm, lt), (um, ut), g, inc_u, c, along, across)
    add_near(2, ints, kept, (lm, lt), (vm, vt), g, inc_v, c, along, across)
    read_slots(far_slots, ints)

    def step(indices):
        for k in indices:
            bins, first, second = decode(kept[k])
            covariance((um, ut), (vm, vt), first, second, along[bins], across, far.at[k])

    in_twos(compact(ints, lambda entry: entry > 0, kept), step)


def far_kernel(group, far_slots, far, inc, g, out, total, ints, kept):
    read_slots(far_slots, ints)
    total[...] = inc[...]

    def step(indices):
        pairs = [decode(kept[k])[1:] for k in indices]
        if group == 1:
            parts = [to_first(g[second], far[k]) for k, (_, second) in zip(indices, pairs)]
            places = [first for first, _ in pairs]
        else:
            parts = [to_second(g[first], far[k]) for k, (first, _) in zip(indices, pairs)]
            places = [second for _, second in pairs]
        for part, here in zip(parts, places):
            total[here] = total[here] + part

    in_twos(compact(ints, lambda entry: entry > 0, kept), step)
    out[...] = total[...].astype(BF16)


def late_kernel(near, lm, lt, um, ut, vm, vt, g_l, g_u, g_v, out, c, along, across, ints, kept):
    tiles, members, points = g_l.shape
    read_slots(near, ints)
    fill_weights(along, across, points)

    def own(k, carry):
        for q in range(2):
            covariance((lm, lt), (lm, lt), 2 * k + q, 2 * k + q, along[0], across, c.at[q])
        for q in range(2):
            t = 2 * k + q
            out[t] = both((lm,), t, range(points // ROWS), points // ROWS).astype(F32) + to_first(g_l[t], c[q])
        return carry

    lax.fori_loop(0, tiles // 2, own, 0)

    for group, right, g in ((0, (lm, lt), g_l), (1, (um, ut), g_u), (2, (vm, vt), g_v)):

        def wanted(entry):
            _, _, second = decode(entry)
            return (entry > 0) & (second >= group * tiles) & (second < (group + 1) * tiles)

        def step(indices):
            pairs = [decode(kept[k]) for k in indices]
            for q, (bins, first, second) in enumerate(pairs):
                covariance((lm, lt), right, first, second - group * tiles, along[bins], across, c.at[q])
            parts = [to_first(g[second - group * tiles], c[q]) for q, (_, _, second) in enumerate(pairs)]
            places = [first for _, first, _ in pairs]
            if group == 0:
                parts += [to_second(g_l[first], c[q]) for q, (_, first, _) in enumerate(pairs)]
                places += [second for _, _, second in pairs]
            for part, here in zip(parts, places):
                out[here] = out[here] + part

        in_twos(compact(ints, wanted, kept), step)


def final_kernel(total, from_u, from_v, out, done, sems):
    copies = []
    for t in range(total.shape[0]):
        done[t] = (total[t] + from_u[t].astype(F32) + from_v[t].astype(F32)).astype(BF16)
        copies.append(pltpu.make_async_copy(done.at[t], out.at[t], sems.at[t]))
        copies[-1].start()
    for copy in copies:
        copy.wait()


def call(kernel, outs, places, scratch, us, *args, grant=VMEM_BYTES, to="v"):
    spec = {"s": pl.BlockSpec(memory_space=pltpu.SMEM), "v": pl.BlockSpec(memory_space=pltpu.VMEM), "h": pl.BlockSpec(memory_space=pl.ANY), "d": pl.BlockSpec(memory_space=pltpu.HBM)}
    return pl.pallas_call(
        kernel,
        out_shape=outs,
        in_specs=[spec[p] for p in places],
        out_specs=jax.tree.map(lambda _: spec[to], outs),
        scratch_shapes=scratch,
        compiler_params=pltpu.CompilerParams(vmem_limit_bytes=grant),
        cost_estimate=pl.CostEstimate(flops=int(us * 1e7), bytes_accessed=int(us * 3e4), transcendentals=0),
    )(*args)


def per_device(anomalies, innovations, obs_tile, pair_tiles, loc_bin):
    tiles, members, points = anomalies.shape
    slots = loc_bin.shape[0]
    size = lax.axis_size("tile")
    place = lax.axis_index("tile")
    core = lax.axis_index("mem")
    routes_u, routes_v = routes(size, FROM_U), routes(size, FROM_V)
    to_u = routes_u + [(size + a, size + b) for a, b in routes_v]
    to_v = routes_v + [(size + a, size + b) for a, b in routes_u]
    send = lambda x, pairs: lax.ppermute(x, ("mem", "tile"), pairs)
    stay = lambda x: pltpu.with_memory_space_constraint(x, pltpu.HBM)
    swap = lambda x: lax.ppermute(x, "mem", [(0, 1), (1, 0)])

    sds = jax.ShapeDtypeStruct
    vm = pltpu.VMEM
    a_l = call(
        pack_kernel,
        sds((tiles * members * (points // ROWS) + SLOT_ROWS, ROWS), BF16),
        "hhh",
        [
            pltpu.SMEM((2, slots), jnp.int32),
            pltpu.SMEM((slots,), jnp.int32),
            pltpu.SemaphoreType.DMA((tiles * (points // ROWS) + 2,)),
        ],
        1,
        stay(pair_tiles.T),
        stay(loc_bin),
        stay(anomalies),
    )
    a_v = send(a_l, to_v)
    a_u = send(a_l, to_u)
    a_t = swap(a_l)
    obs_tile, a_t = lax.optimization_barrier((obs_tile, a_t))
    forcing = call(
        forcing_kernel, sds(anomalies.shape, BF16), "sv", [vm(anomalies.shape, F32)], 1, obs_tile, stay(innovations)
    )
    g_v = send(forcing, to_v)
    late_forcing, a_v = lax.optimization_barrier((forcing, a_v))
    g_u = send(late_forcing, to_u)
    other_list = jnp.where((place % 4 != 2) == (core == 0), slot_codes(a_u, slots), slot_codes(a_v, slots))
    near, far_slots = entries_for(slot_codes(a_l, slots), other_list, place, core, tiles)
    square = vm((points, points), BF16)
    across = vm((points // WIDTH, points), F32)
    weights = [square, vm((NBIN, WIDTH, points), F32), across]
    weights_far = [vm((2, points, points), BF16), vm((2 * NBIN, WIDTH, points), F32), across]
    ints = pltpu.SMEM((slots,), jnp.int32)

    a_vt = swap(a_u)
    a_ut = swap(a_v)
    far, inc_u, inc_v = call(
        early_kernel,
        (sds((slots, points, points), BF16), sds(anomalies.shape, F32), sds(anomalies.shape, F32)),
        "vvvvvvvvv",
        [*weights_far, ints, ints],
        4,
        near,
        far_slots,
        a_l,
        a_t,
        a_u,
        a_ut,
        a_v,
        a_vt,
        forcing,
    )
    finish = lambda group, inc, g: call(
        functools.partial(far_kernel, group),
        sds(anomalies.shape, BF16),
        "vvvv",
        [vm(anomalies.shape, F32), ints, ints],
        1,
        far_slots,
        far,
        inc,
        g,
    )
    from_u = send(finish(1, inc_u, g_v), back(to_u))
    from_v = send(finish(2, inc_v, g_u), back(to_v))
    total = call(
        late_kernel,
        sds(anomalies.shape, F32),
        "vvvvvvvvvv",
        [vm((2, points, points), BF16), *weights[1:], ints, ints],
        10,
        near,
        a_l,
        a_t,
        a_u,
        a_ut,
        a_v,
        a_vt,
        forcing,
        g_u,
        g_v,
    )
    return call(
        final_kernel,
        sds(anomalies.shape, BF16),
        "vvv",
        [vm(anomalies.shape, BF16), pltpu.SemaphoreType.DMA((tiles,))],
        1,
        total,
        from_v,
        from_u,
        to="h",
    )


def solution(mesh):
    return jax.shard_map(
        per_device,
        mesh=mesh,
        in_specs=(
            P("tile", "mem", None),
            P("tile", "mem", None),
            P("tile"),
            P("tile", None),
            P("tile"),
        ),
        out_specs=P("tile", "mem", None),
        check_vma=False,
    )
```
